32 devices in a mesh: groups: 2 (over y), tensor: 4 (over z), store: 4 (over x, core).
Axes of the slice: x: 2, y: 2, z: 4, core: 2. Of those that a mesh axis runs over, the one named last changes fastest.
Arguments:
- tokens: bfloat16 [4096, 8192], P(('groups', 'store', 'tensor')), parts along dimension 0, may hold values from -32 to 32
- query_weight: bfloat16 [8192, 8192], P(None, 'tensor'), may hold values from -0.0625 to 0.0625
- key_value_weight: bfloat16 [8192, 2048], P(None, 'tensor'), may hold values from -0.0625 to 0.0625
- adapter_down_maps: bfloat16 [32, 128, 8192], P('store', None, 'tensor'), may hold values from -0.0625 to 0.0625
- adapter_up_query: bfloat16 [32, 64, 8192], P('store', None, 'tensor'), may hold values from -0.375 to 0.375
- adapter_up_key_value: bfloat16 [32, 64, 2048], P('store', None, 'tensor'), may hold values from -0.375 to 0.375
- adapter_row_table: int32 [64], P('groups'), parts along dimension 0, may hold values from 0 to 31, as said below
- request_adapter_ids: int32 [8, 4], P('groups'), parts along dimension 0, may hold values from 0 to 31, as said below
- token_request_ids: int32 [8, 512], P(('groups', 'store')), parts along dimension 0, may hold values from 0 to 3, never falling along the last dimension, each value on 1 to 256 neighbouring positions
Outputs:
- attention: bfloat16 [4096, 8192], P(('groups', 'store'), 'tensor'), parts along dimension 0
The draws below stay inside these ranges and needn't reach their ends.
There are 2 independent parts, one for each index of `groups`. The reference program is written for one: setup_inputs(seed, part) draws one part's arguments, and reference() takes and returns one part's arrays. A program takes and returns all parts, laid end to end along the dimension named above; an argument that names none is the same for every part. Nothing has to cross between parts.
Inputs may be any that keep to these rules, and one draw needn't show every extreme that they name: A permutation: adapter a lies in row adapter_row_table[a] of the adapter arrays, on store index adapter_row_table[a] // 8. `request_adapter_ids`: the 4 requests of one store batch use adapters held on 4 different store indices. `token_request_ids`: requests are contiguous runs of a store batch, each of 1 to 256 tokens.
All inputs are finite; a program needn't handle non-finite values.
Results may differ from the reference program's by a relative error of at most 0.012.
The reference program's roundings to bfloat16 on the way (of `low`, `query`, `keys`, `values` and `weights`) count: a program that leaves them out, or rounds other values in their place, can miss the bound.
Values may be sent and summed in bfloat16 or wider, within the bound.
No kernel may reach another device: no remote copies, remote signals or barrier semaphores. Data moves between devices by JAX's collectives and lax.ppermute only.
A program may use at most 128 MiB of HBM per device.

```python
import math
import jax
import jax.numpy as jnp
import numpy as np
from jax import lax

MODEL_WIDTH = 8192
QUERY_HEADS = 64
KEY_VALUE_HEADS = 8
HEAD_SIZE = 128
ADAPTER_RANK = 64
STORE_REQUESTS = 4
TOK_ST = 512
SLOTS = 8
TOKENS = 2048
ADAPTER_COUNT = 32
N_TENSOR = 4
N_STORE = 4


def draw_tokens(key, part):
    values = jnp.clip(jax.random.normal(jax.random.fold_in(key, 3), (TOKENS, MODEL_WIDTH), jnp.float32), -4.0, 4.0)
    return values.astype(jnp.bfloat16)


def place_slot(owners, locals_table, row_pick, col_pick, slot_value):
    target = slot_value // SLOTS
    row_index = jnp.arange(N_STORE, dtype=jnp.int32)[:, None]
    col_index = jnp.arange(N_STORE, dtype=jnp.int32)[None, :]
    in_row = row_index == row_pick
    current = owners[row_pick, col_pick]
    moved = jnp.where(in_row & (owners == target), current, owners)
    moved = jnp.where(in_row & (col_index == col_pick), target, moved)
    locals_new = jnp.where(in_row & (col_index == col_pick), slot_value % SLOTS, locals_table)
    return (moved, locals_new)


def owner_rows(row_key):
    return jax.random.permutation(row_key, N_STORE).astype(jnp.int32)


def placement_tables(key):
    adapter_total = SLOTS * N_STORE
    order = jax.random.permutation(jax.random.fold_in(key, 21), adapter_total).astype(jnp.int32)
    inverse = jnp.zeros((adapter_total,), jnp.int32).at[order].set(jnp.arange(adapter_total, dtype=jnp.int32))
    row_keys = jax.random.split(jax.random.fold_in(key, 22), N_STORE)
    owners = jax.vmap(owner_rows)(row_keys)
    locals_table = jax.random.randint(jax.random.fold_in(key, 23), (N_STORE, N_STORE), 0, SLOTS).astype(jnp.int32)
    first_row = jax.random.randint(jax.random.fold_in(key, 24), (), 0, N_STORE).astype(jnp.int32)
    second_row = ((first_row + 1 + jax.random.randint(jax.random.fold_in(key, 25), (), 0, N_STORE - 1)) % N_STORE).astype(jnp.int32)
    first_col = jax.random.randint(jax.random.fold_in(key, 26), (), 0, STORE_REQUESTS).astype(jnp.int32)
    second_col = jax.random.randint(jax.random.fold_in(key, 27), (), 0, STORE_REQUESTS).astype(jnp.int32)
    owners, locals_table = place_slot(owners, locals_table, first_row, first_col, order[adapter_total - 1])
    owners, locals_table = place_slot(owners, locals_table, second_row, second_col, order[0])
    positions_list = owners[:, :STORE_REQUESTS] * SLOTS + locals_table[:, :STORE_REQUESTS]
    return (order, inverse[positions_list].astype(jnp.int32))


def draw_adapter_row_table(key, part):
    return placement_tables(key)[0]


def draw_request_adapter_ids(key, part):
    return placement_tables(key)[1]


def steps_of(own_key, shape, shards, smallest, top_value):
    def one(axis_at, shards_of):
        draws = jax.random.uniform(jax.random.fold_in(jax.random.fold_in(own_key, 6), axis_at), (shards_of,), jnp.float32, smallest / len(shards), top_value / len(shards))
        return jnp.repeat(jnp.exp(draws), shape[axis_at] // shards_of).reshape((-1,) + (1,) * (len(shape) - axis_at - 1))

    loudness = one(*shards[0])
    for cut in shards[1:]:
        loudness = loudness * one(*cut)
    return loudness


def length_profile(count, total, limit, skew):
    weights = [(1 << 20) // math.isqrt(standing ** skew) + 1 for standing in range(2, count + 1)]
    surplus, holding = total - limit - (count - 1), [1] * (count - 1)
    while surplus > 0:
        candidates = [i for i in range(count - 1) if holding[i] < limit]
        mass, remaining = sum([weights[i] for i in candidates]), surplus
        for i in candidates:
            extra = min(limit - holding[i], max(1, remaining * weights[i] // mass), surplus)
            holding[i] = holding[i] + extra
            surplus = surplus - extra
    return np.array([limit] + holding)


def uneven_parts(rng, amount, total, bound, skew):
    if amount == 2:
        one = jax.random.randint(rng, (), max(1, total - bound), min(bound, total - 1) + 1)
        return jnp.stack([one, total - one])
    tallies = jnp.asarray(length_profile(amount, total, bound, skew), jnp.int32)
    couples = (amount - 1) // 2
    giver, taker = tallies[1:1 + 2 * couples:2], tallies[2:2 + 2 * couples:2]
    slack = jnp.minimum(giver - 1, bound - taker)
    passed = jax.random.randint(jax.random.fold_in(rng, 1), (couples,), 0, 1 << 20) % (slack + 1)
    tallies = tallies.at[1:1 + 2 * couples:2].set(giver - passed).at[2:2 + 2 * couples:2].set(taker + passed)
    return tallies[jax.random.permutation(jax.random.fold_in(rng, 2), amount)]


def noise(rng, shape, scale, bound, pieces=(), held_as=jnp.bfloat16):
    values = scale * jax.random.normal(rng, shape, jnp.float32)
    if pieces:
        values = values * steps_of(rng, shape, pieces, -0.22, 0.18)
    return jnp.clip(values, -bound, bound).astype(held_as)


def setup_inputs(seed: int = 0, part: int = 0) -> dict:
    seeds = jax.random.split(jax.random.key(seed), 10)
    part_splits = jax.random.split(jax.random.fold_in(seeds[9], part), 10)
    return {
        "tokens": draw_tokens(jax.random.fold_in(jax.random.fold_in(seeds[9], part), 71), part),
        "query_weight": noise(seeds[1], (MODEL_WIDTH, QUERY_HEADS * HEAD_SIZE), MODEL_WIDTH ** -0.5, 0.0625, ((1, 4),)),
        "key_value_weight": noise(seeds[2], (MODEL_WIDTH, 2 * KEY_VALUE_HEADS * HEAD_SIZE), MODEL_WIDTH ** -0.5, 0.0625, ((1, 4),)),
        "adapter_down_maps": noise(seeds[3], (ADAPTER_COUNT, 2 * ADAPTER_RANK, MODEL_WIDTH), MODEL_WIDTH ** -0.5, 0.0625, ((0, 4), (2, 4))),
        "adapter_up_query": noise(seeds[4], (ADAPTER_COUNT, ADAPTER_RANK, QUERY_HEADS * HEAD_SIZE), (4 * ADAPTER_RANK) ** -0.5, 0.375, ((0, 4), (2, 4))),
        "adapter_up_key_value": noise(seeds[5], (ADAPTER_COUNT, ADAPTER_RANK, 2 * KEY_VALUE_HEADS * HEAD_SIZE), (4 * ADAPTER_RANK) ** -0.5, 0.375, ((0, 4), (2, 4))),
        "adapter_row_table": draw_adapter_row_table(jax.random.fold_in(jax.random.fold_in(seeds[9], part), 71), part),
        "request_adapter_ids": draw_request_adapter_ids(jax.random.fold_in(jax.random.fold_in(seeds[9], part), 71), part),
        "token_request_ids": jax.vmap(lambda own: jnp.searchsorted(jnp.cumsum(uneven_parts(own, STORE_REQUESTS, TOK_ST, TOK_ST // 2, 2)), jnp.arange(TOK_ST), side="right"))(jax.random.split(part_splits[8], N_STORE)).reshape((N_STORE, TOK_ST)).astype(jnp.int32),
    }


adapter_scale = 2.0
rope_theta = 500000.0

def token_positions(segment_row):
    members = segment_row[:, None] == jnp.arange(STORE_REQUESTS, dtype=jnp.int32)[None, :]
    counts = lax.optimization_barrier(jnp.sum(members.astype(jnp.int32), axis=0)).astype(jnp.int32)
    starts = (jnp.cumsum(counts) - counts).astype(jnp.int32)
    first_index = lax.optimization_barrier(jnp.sum(jnp.where(members, starts[None, :], 0), axis=1)).astype(jnp.int32)
    return jnp.arange(segment_row.shape[0], dtype=jnp.int32) - first_index

def rotary(heads_values, positions):
    half_size = heads_values.shape[-1] // 2
    exponent = jnp.arange(half_size, dtype=jnp.float32) * (2.0 / heads_values.shape[-1])
    frequency = jnp.exp(-exponent * math.log(rope_theta))
    angles = positions.astype(jnp.float32)[:, None] * frequency[None, :]
    cosine = jnp.cos(angles)[:, None, :]
    sine = jnp.sin(angles)[:, None, :]
    lower = heads_values[..., :half_size]
    upper = heads_values[..., half_size:]
    return jnp.concatenate([lower * cosine - upper * sine, upper * cosine + lower * sine], axis=-1)

def reference(tokens, query_weight, key_value_weight, adapter_down_maps, adapter_up_query, adapter_up_key_value, adapter_row_table, request_adapter_ids, token_request_ids):
    group_size = QUERY_HEADS // KEY_VALUE_HEADS
    pair_count = N_TENSOR // 2
    pair_heads = 2 * KEY_VALUE_HEADS // N_TENSOR
    slot_table = adapter_row_table[request_adapter_ids].astype(jnp.int32)
    batches = tokens.reshape(N_STORE, TOK_ST, MODEL_WIDTH)

    def one_batch(inputs):
        gathered_rows, positions_list, segment_row = inputs
        members = segment_row[:, None] == jnp.arange(STORE_REQUESTS, dtype=jnp.int32)[None, :]
        member_float = members.astype(jnp.float32)
        member_half = members.astype(jnp.bfloat16)
        down_product = adapter_down_maps[positions_list].astype(jnp.float32)
        projected = jnp.einsum('td,krd->tkr', gathered_rows.astype(jnp.float32), down_product)
        low = lax.optimization_barrier(jnp.sum(projected * member_float[:, :, None], axis=1)).astype(jnp.bfloat16)
        token_query_update = (low[:, None, :ADAPTER_RANK] * member_half[:, :, None]).reshape(TOK_ST, STORE_REQUESTS * ADAPTER_RANK)
        token_key_value_update = (low[:, None, ADAPTER_RANK:] * member_half[:, :, None]).reshape(TOK_ST, STORE_REQUESTS * ADAPTER_RANK)
        query_update = jnp.dot(token_query_update, adapter_up_query[positions_list].reshape(STORE_REQUESTS * ADAPTER_RANK, QUERY_HEADS * HEAD_SIZE), preferred_element_type=jnp.float32)
        key_value_update = jnp.dot(token_key_value_update, adapter_up_key_value[positions_list].reshape(STORE_REQUESTS * ADAPTER_RANK, 2 * KEY_VALUE_HEADS * HEAD_SIZE), preferred_element_type=jnp.float32)
        query_unrotated = jnp.dot(gathered_rows, query_weight, preferred_element_type=jnp.float32) + adapter_scale * query_update
        key_value_unrotated = jnp.dot(gathered_rows, key_value_weight, preferred_element_type=jnp.float32) + adapter_scale * key_value_update
        positions = token_positions(segment_row)
        query = rotary(query_unrotated.reshape(TOK_ST, QUERY_HEADS, HEAD_SIZE), positions).astype(jnp.bfloat16)
        keyval = key_value_unrotated.reshape(TOK_ST, pair_count, 2, pair_heads, HEAD_SIZE)
        keys = rotary(keyval[:, :, 0].reshape(TOK_ST, KEY_VALUE_HEADS, HEAD_SIZE), positions).astype(jnp.bfloat16)
        values = keyval[:, :, 1].reshape(TOK_ST, KEY_VALUE_HEADS, HEAD_SIZE).astype(jnp.bfloat16)
        grouped = query.reshape(TOK_ST, KEY_VALUE_HEADS, group_size, HEAD_SIZE)
        scores = jnp.einsum('tkgd,skd->kgts', grouped.astype(jnp.float32), keys.astype(jnp.float32)) / math.sqrt(HEAD_SIZE)
        token_index = jnp.arange(TOK_ST, dtype=jnp.int32)
        allowed = (segment_row[:, None] == segment_row[None, :]) & (token_index[:, None] >= token_index[None, :])
        scores = jnp.where(allowed, scores, -1e+30)
        scores = scores - lax.optimization_barrier(jnp.max(scores, axis=-1, keepdims=True))
        weights = jnp.exp(scores)
        weights = (weights / lax.optimization_barrier(jnp.sum(weights, axis=-1, keepdims=True))).astype(jnp.bfloat16)
        mixed = jnp.einsum('kgts,skd->tkgd', weights.astype(jnp.float32), values.astype(jnp.float32))
        return mixed.reshape(TOK_ST, QUERY_HEADS * HEAD_SIZE).astype(jnp.bfloat16)
    result = lax.map(one_batch, (batches, slot_table, token_request_ids))
    return result.reshape(TOKENS, QUERY_HEADS * HEAD_SIZE)
```

```python
import functools
import math

import jax
import jax.numpy as jnp
from jax import lax
from jax.experimental import pallas as pl
from jax.experimental.pallas import tpu as pltpu
from jax.sharding import PartitionSpec as P

QUERY_HEADS = 64
KEY_VALUE_HEADS = 8
HEAD_SIZE = 128
ADAPTER_RANK = 64
STORE_REQUESTS = 4
LONGEST_REQUEST = 256

adapter_scale = 2.0
rope_theta = 500000.0

CHUNKS = 4
TILE = 128
VMEM_LIMIT = 40 * 2**20
F32 = jnp.float32
BF16 = jnp.bfloat16
ANY = pl.BlockSpec(memory_space=pl.ANY)


def params():
    return pltpu.CompilerParams(vmem_limit_bytes=VMEM_LIMIT)


def whole(shape):
    return pl.BlockSpec(shape, lambda *_: (0,) * len(shape))


def start_picked(candidates, pick, target, semaphore, columns=None):
    def start(source):
        view = source if columns is None else source.at[:, columns]
        pltpu.make_async_copy(view, target, semaphore).start()

    if len(candidates) == 1:
        start(candidates[0])
        return
    for index, source in enumerate(candidates):
        pl.when(pick == index)(functools.partial(start, source))


def project(candidates, picks, chunk_ids, weights, starts=None):
    steps, groups = len(candidates), len(candidates[0])
    rows, chunk = candidates[0][0][0].shape
    block = min(1024, chunk)
    sub = chunk // block
    flat = [x for at_chunk in candidates for group in at_chunk for x in group]
    widths = [w.shape[1] for w in weights]
    count = len(weights)

    def kernel(info, *refs):
        tokens_in = iter(refs[: len(flat)])
        sources = [[[next(tokens_in) for _ in group] for group in at_chunk] for at_chunk in candidates]
        rest = refs[len(flat) :]
        weight_refs, rest = rest[:count], rest[count:]
        start_refs = ()
        if starts is not None:
            start_refs, rest = rest[:count], rest[count:]
        out_refs, (held, sems) = rest[:count], rest[count:]
        step = pl.program_id(0)
        at = step // sub

        @pl.when(step == 0)
        def _():
            for a in range(steps):
                for r in range(groups):
                    start_picked(
                        sources[a][r], info[r], held.at[a, pl.ds(r * rows, rows), :], sems.at[a, r]
                    )

        @pl.when(step % sub == 0)
        def _():
            for r in range(groups):
                pltpu.make_async_copy(
                    sources[0][r][0], held.at[at, pl.ds(r * rows, rows), :], sems.at[at, r]
                ).wait()

        part = held[at, :, pl.ds(pl.multiple_of((step % sub) * block, block), block)]
        for i in range(count):
            product = jnp.dot(part, weight_refs[i][...], preferred_element_type=F32)

            @pl.when(step == 0)
            def _(i=i, product=product):
                out_refs[i][...] = product if starts is None else start_refs[i][...] + product

            @pl.when(step > 0)
            def _(i=i, product=product):
                out_refs[i][...] += product

    height = groups * rows
    info = jnp.concatenate([jnp.asarray(picks, jnp.int32), jnp.asarray(chunk_ids, jnp.int32)])
    results = pl.pallas_call(
        kernel,
        grid_spec=pltpu.PrefetchScalarGridSpec(
            num_scalar_prefetch=1,
            grid=(steps * sub,),
            in_specs=[ANY] * len(flat)
            + [
                pl.BlockSpec(
                    (block, w), lambda g, info: (info[groups + g // sub] * sub + g % sub, 0)
                )
                for w in widths
            ]
            + ([whole((height, w)) for w in widths] if starts is not None else []),
            out_specs=[whole((height, w)) for w in widths],
            scratch_shapes=[
                pltpu.VMEM((steps, height, chunk), BF16),
                pltpu.SemaphoreType.DMA((steps, groups)),
            ],
        ),
        out_shape=[jax.ShapeDtypeStruct((height, w), F32) for w in widths],
        compiler_params=params(),
        cost_estimate=pl.CostEstimate(
            flops=2 * height * steps * chunk * sum(widths),
            bytes_accessed=2 * steps * chunk * (sum(widths) + height),
            transcendentals=0,
        ),
    )(info, *flat, *weights, *(starts or []))
    return results


def low_parts(candidates, pick, offset, width, downs, member_groups):
    groups = len(candidates)
    rows = candidates[0][0].shape[0]
    flat = [x for group in candidates for x in group]
    holders = len(downs)
    rank = downs[0].shape[0]
    members = jnp.concatenate(member_groups, axis=0)

    def kernel(info, *refs):
        tokens_in = iter(refs[: len(flat)])
        sources = [[next(tokens_in) for _ in group] for group in candidates]
        down_refs = refs[len(flat) : len(flat) + holders]
        member_ref, out_ref, held, sems = refs[len(flat) + holders :]
        columns = pl.ds(pl.multiple_of(info[1], 128), width)
        for r in range(groups):
            start_picked(sources[r], info[0], held.at[pl.ds(r * rows, rows), :], sems.at[r], columns)
        for r in range(groups):
            pltpu.make_async_copy(
                sources[r][0].at[:, columns], held.at[pl.ds(r * rows, rows), :], sems.at[r]
            ).wait()
        total = None
        for d in range(holders):
            product = lax.dot_general(
                held[...], down_refs[d][...], (((1,), (1,)), ((), ())), preferred_element_type=F32
            )
            term = product * member_ref[:, d : d + 1]
            total = term if total is None else total + term
        out_ref[...] = total

    return pl.pallas_call(
        kernel,
        grid_spec=pltpu.PrefetchScalarGridSpec(
            num_scalar_prefetch=1,
            grid=(1,),
            in_specs=[ANY] * len(flat)
            + [whole(d.shape) for d in downs]
            + [whole(members.shape)],
            out_specs=whole((groups * rows, rank)),
            scratch_shapes=[
                pltpu.VMEM((groups * rows, width), BF16),
                pltpu.SemaphoreType.DMA((groups,)),
            ],
        ),
        out_shape=jax.ShapeDtypeStruct((groups * rows, rank), F32),
        compiler_params=params(),
        cost_estimate=pl.CostEstimate(
            flops=2 * groups * rows * width * rank * holders,
            bytes_accessed=2 * width * (groups * rows + rank * holders),
            transcendentals=0,
        ),
    )(jnp.stack([pick, offset]).astype(jnp.int32), *flat, *downs, members)


def spread(low, member):
    return jnp.concatenate([low * member[:, d : d + 1] for d in range(member.shape[1])], axis=1)


def rotate(block, cosine, sine):
    return block * cosine + pltpu.roll(block, HEAD_SIZE // 2, 1) * sine


def finish(sources, rank_index, low, members, up_query, up_keyval, tables, firsts, blocks):
    rows = low.shape[0] // blocks
    query_width = up_query.shape[1]
    keyval_width = up_keyval.shape[1]
    used = firsts[2] * HEAD_SIZE
    rank = ADAPTER_RANK
    count = len(sources)

    def kernel(info, *refs):
        sums = refs[: 2 * count]
        (low_ref, member_ref, upq_ref, upkv_ref, cos_ref, sin_ref, kcos_ref, ksin_ref) = refs[
            2 * count : 2 * count + 8
        ]
        query_ref, mine_ref, send_ref, held_q, held_kv, sems = refs[2 * count + 8 :]
        block = pl.program_id(0)
        z = info[0]
        for i, (_, _, first, test) in enumerate(sources):

            @pl.when(test(block, z))
            def _(i=i, first=first):
                a = pltpu.make_async_copy(sums[2 * i].at[pl.ds(first, rows), :], held_q, sems.at[0])
                b = pltpu.make_async_copy(
                    sums[2 * i + 1].at[pl.ds(first, rows), :], held_kv, sems.at[1]
                )
                a.start()
                b.start()
                a.wait()
                b.wait()

        member = member_ref[...].astype(BF16)
        low_block = low_ref[...]
        update = jnp.dot(
            spread(low_block[:, :rank], member), upq_ref[...], preferred_element_type=F32
        )
        for h in range(query_width // HEAD_SIZE):
            at = slice(h * HEAD_SIZE, (h + 1) * HEAD_SIZE)
            query_ref[:, at] = rotate(
                held_q[:, at] + adapter_scale * update[:, at], cos_ref[...], sin_ref[...]
            ).astype(BF16)
        update = jnp.dot(
            spread(low_block[:, rank:], member), upkv_ref[...], preferred_element_type=F32
        )
        for h in range(keyval_width // HEAD_SIZE):
            at = slice(h * HEAD_SIZE, (h + 1) * HEAD_SIZE)
            held_kv[:, at] = rotate(
                held_kv[:, at] + adapter_scale * update[:, at], kcos_ref[...], ksin_ref[...]
            )
        mine_ref[...] = held_kv[:, pl.ds(pl.multiple_of(info[1], HEAD_SIZE), used)].astype(BF16)
        send_ref[...] = held_kv[:, pl.ds(pl.multiple_of(info[2], HEAD_SIZE), used)].astype(BF16)

    def by_block(width):
        return pl.BlockSpec((rows, width), lambda b, info: (b, 0))

    flat = [x for q, kv, _, _ in sources for x in (q, kv)]
    total = rows * blocks
    info = jnp.stack([rank_index, firsts[0] * HEAD_SIZE, firsts[1] * HEAD_SIZE]).astype(jnp.int32)
    return pl.pallas_call(
        kernel,
        grid_spec=pltpu.PrefetchScalarGridSpec(
            num_scalar_prefetch=1,
            grid=(blocks,),
            in_specs=[ANY] * len(flat)
            + [
                by_block(low.shape[1]),
                by_block(members.shape[1]),
                whole(up_query.shape),
                whole(up_keyval.shape),
            ]
            + [by_block(HEAD_SIZE)] * 4,
            out_specs=[by_block(query_width), by_block(used), by_block(used)],
            scratch_shapes=[
                pltpu.VMEM((rows, query_width), F32),
                pltpu.VMEM((rows, keyval_width), F32),
                pltpu.SemaphoreType.DMA((2,)),
            ],
        ),
        out_shape=[
            jax.ShapeDtypeStruct((total, query_width), BF16),
            jax.ShapeDtypeStruct((total, used), BF16),
            jax.ShapeDtypeStruct((total, used), BF16),
        ],
        compiler_params=params(),
        cost_estimate=pl.CostEstimate(
            flops=2 * total * up_query.shape[0] * (query_width + keyval_width),
            bytes_accessed=8 * total * (query_width + keyval_width),
            transcendentals=0,
        ),
    )(info, *flat, low, members, up_query, up_keyval, *tables)


def finish_late(candidates, pick, chunk_id, weight, sums, low, member, up, cosine, sine, cuts=None):
    rows, chunk = candidates[0].shape
    width = weight.shape[1]
    step_width = min(512, width)
    steps = width // step_width
    count = len(candidates)

    def kernel(info, *refs):
        sources = refs[:count]
        weight_ref, sum_ref, low_ref, member_ref, up_ref, cos_ref, sin_ref = refs[count : count + 7]
        rest = refs[count + 7 :]
        outs, (held, sem) = rest[:-2], rest[-2:]

        @pl.when(pl.program_id(0) == 0)
        def _():
            start_picked(sources, info[0], held, sem.at[0])
            pltpu.make_async_copy(sources[0], held, sem.at[0]).wait()

        update = jnp.dot(
            spread(low_ref[...], member_ref[...].astype(BF16)),
            up_ref[...],
            preferred_element_type=F32,
        )
        raw = (
            jnp.dot(held[...], weight_ref[...], preferred_element_type=F32)
            + sum_ref[...]
            + adapter_scale * update
        )
        parts = [
            rotate(raw[:, h * HEAD_SIZE : (h + 1) * HEAD_SIZE], cos_ref[...], sin_ref[...])
            for h in range(step_width // HEAD_SIZE)
        ]
        if cuts is None:
            for h, part in enumerate(parts):
                outs[0][:, h * HEAD_SIZE : (h + 1) * HEAD_SIZE] = part.astype(BF16)
        else:
            for out, first in ((outs[0], info[2]), (outs[1], info[3])):
                for u in range(cuts[2]):
                    chosen = parts[0]
                    for h in range(1, len(parts)):
                        chosen = jnp.where(first + u == h, parts[h], chosen)
                    out[:, u * HEAD_SIZE : (u + 1) * HEAD_SIZE] = chosen.astype(BF16)

    def column(height):
        return pl.BlockSpec((height, step_width), lambda g, info: (0, g))

    if cuts is None:
        outs = [jax.ShapeDtypeStruct((rows, width), BF16)]
        out_specs = [column(rows)]
        info = [pick, chunk_id]
    else:
        used = cuts[2] * HEAD_SIZE
        outs = [jax.ShapeDtypeStruct((rows, used), BF16)] * 2
        out_specs = [whole((rows, used))] * 2
        info = [pick, chunk_id, cuts[0], cuts[1]]
    return pl.pallas_call(
        kernel,
        grid_spec=pltpu.PrefetchScalarGridSpec(
            num_scalar_prefetch=1,
            grid=(steps,),
            in_specs=[ANY] * count
            + [
                pl.BlockSpec((chunk, step_width), lambda g, info: (info[1], g)),
                column(rows),
                whole(low.shape),
                whole(member.shape),
                column(up.shape[0]),
                whole(cosine.shape),
                whole(sine.shape),
            ],
            out_specs=out_specs,
            scratch_shapes=[pltpu.VMEM((rows, chunk), BF16), pltpu.SemaphoreType.DMA((1,))],
        ),
        out_shape=outs,
        compiler_params=params(),
        cost_estimate=pl.CostEstimate(
            flops=2 * rows * width * (chunk + up.shape[0]),
            bytes_accessed=2 * width * chunk,
            transcendentals=0,
        ),
    )(jnp.stack(info).astype(jnp.int32), *candidates, weight, sums, low, member, up, cosine, sine)


def attend(query, query_late, mine, mine_late, recv, recv_late, ids_column, ids_row, info, blocks):
    total, width = query.shape
    rows = total // blocks
    heads = width // HEAD_SIZE
    used = mine.shape[1] // HEAD_SIZE
    per_kv = heads // used
    together = min(4, per_kv)
    span = together * HEAD_SIZE
    scale = math.log2(math.e) / math.sqrt(HEAD_SIZE)
    tiles = total // TILE
    back = -(-(LONGEST_REQUEST - 1) // TILE)

    def kernel(info, q_ref, ql_ref, m_ref, ml_ref, r_ref, rl_ref, idc_ref, idr_ref, out_ref, k_ref, v_ref):
        step = pl.program_id(0)

        @pl.when(step == 0)
        def _():
            def put(keys_mine):
                own, other = (k_ref, v_ref) if keys_mine else (v_ref, k_ref)
                own[...] = m_ref[...]
                other[...] = r_ref[...]

                @pl.when(info[0] >= 0)
                def _():
                    own[pl.ds(pl.multiple_of(info[0], rows), rows), :] = ml_ref[...]

                @pl.when(info[1] >= 0)
                def _():
                    other[pl.ds(pl.multiple_of(info[1], rows), rows), :] = rl_ref[...]

            pl.when(info[2] == 1)(lambda: put(True))
            pl.when(info[2] == 0)(lambda: put(False))

        @pl.when(info[0] >= 0)
        def _():
            q_ref[pl.ds(pl.multiple_of(info[0], rows), rows), :] = ql_ref[...]

        kv_at = pl.ds(pl.multiple_of((step * together // per_kv) * HEAD_SIZE, HEAD_SIZE), HEAD_SIZE)
        for tile in range(tiles):
            low_tile = max(0, tile - back)
            key_rows = (tile + 1 - low_tile) * TILE
            at = slice(tile * TILE, (tile + 1) * TILE)
            keys = k_ref[low_tile * TILE : low_tile * TILE + key_rows, kv_at]
            values = v_ref[low_tile * TILE : low_tile * TILE + key_rows, kv_at]
            row_index = lax.broadcasted_iota(jnp.int32, (TILE, key_rows), 0) + tile * TILE
            column_index = lax.broadcasted_iota(jnp.int32, (TILE, key_rows), 1) + low_tile * TILE
            allowed = (idc_ref[at, :] == idr_ref[:, low_tile * TILE : low_tile * TILE + key_rows]) & (
                row_index >= column_index
            )
            for h in range(together):
                query_part = q_ref[at, h * HEAD_SIZE : (h + 1) * HEAD_SIZE]
                scores = lax.dot_general(
                    query_part, keys, (((1,), (1,)), ((), ())), preferred_element_type=F32
                )
                scores = jnp.where(allowed, scores * scale, -1e30)
                top = jnp.max(scores, axis=1, keepdims=True)
                weights = jnp.exp2(scores - top)
                norm = jnp.sum(weights, axis=1, keepdims=True)
                mixed = jnp.dot(weights.astype(BF16), values, preferred_element_type=F32)
                out_ref[at, h * HEAD_SIZE : (h + 1) * HEAD_SIZE] = (mixed * (1.0 / norm)).astype(BF16)

    by_heads = pl.BlockSpec((total, span), lambda g, info: (0, g))
    return pl.pallas_call(
        kernel,
        grid_spec=pltpu.PrefetchScalarGridSpec(
            num_scalar_prefetch=1,
            grid=(heads // together,),
            in_specs=[
                by_heads,
                pl.BlockSpec((rows, span), lambda g, info: (0, g)),
                whole(mine.shape),
                whole(mine_late.shape),
                whole(recv.shape),
                whole(recv_late.shape),
                whole(ids_column.shape),
                whole(ids_row.shape),
            ],
            out_specs=by_heads,
            scratch_shapes=[pltpu.VMEM(mine.shape, BF16), pltpu.VMEM(mine.shape, BF16)],
        ),
        out_shape=jax.ShapeDtypeStruct((total, width), BF16),
        compiler_params=params(),
        cost_estimate=pl.CostEstimate(
            flops=4 * total * total * width,
            bytes_accessed=4 * total * width,
            transcendentals=total * total * heads,
        ),
    )(info, query, query_late, mine, mine_late, recv, recv_late, ids_column, ids_row)


def on_device(
    tokens,
    query_weight,
    key_value_weight,
    adapter_down_maps,
    adapter_up_query,
    adapter_up_key_value,
    adapter_row_table,
    request_adapter_ids,
    token_request_ids,
):
    z = lax.axis_index("tensor")
    store = lax.axis_index("store")
    n = lax.axis_size("tensor")
    stores = lax.axis_size("store")
    rows, model_width = tokens.shape
    total = rows * n
    half = n // 2
    late = n - 1
    chunks = CHUNKS
    chunk_width = model_width // chunks
    width_share = model_width // n
    slices = n // chunks
    home_chunk = z // slices
    home_offset = (z % slices) * width_share
    side = (z >= half).astype(jnp.int32)
    query_width = query_weight.shape[1]
    keyval_width = key_value_weight.shape[1]

    down = {(0, c): tokens[:, c * chunk_width : (c + 1) * chunk_width] for c in range(chunks)}
    up = dict(down)
    for k in range(1, n):
        for a in range(chunks):
            c = a
            down[k, c] = lax.ppermute(
                down[k - 1, c], "tensor", [(i, i - 1) for i in range(1, n - k + 1)]
            )
            c = chunks - 1 - a
            up[k, c] = lax.ppermute(up[k - 1, c], "tensor", [(i, i + 1) for i in range(k - 1, n - 1)])

    per_store = adapter_down_maps.shape[0]
    lookup = (
        request_adapter_ids[:, :, None]
        == jnp.arange(adapter_row_table.shape[0], dtype=jnp.int32)[None, None, :]
    ).astype(jnp.int32)
    slot_table = jnp.sum(lookup * adapter_row_table[None, None, :], axis=2)
    here = slot_table // per_store == store
    local = jnp.sum(jnp.where(here, slot_table - store * per_store, 0), axis=1)

    def exchanged(stack):
        got = []
        for d in range(stores):
            target = (store + d) % stores
            row = lax.dynamic_index_in_dim(local, target, 0, keepdims=False)
            part = lax.dynamic_index_in_dim(stack, row, 0, keepdims=False)
            got.append(
                part
                if d == 0
                else lax.ppermute(part, "store", [(i, (i + d) % stores) for i in range(stores)])
            )
        return got

    downs = exchanged(adapter_down_maps)
    up_query = jnp.concatenate(exchanged(adapter_up_query), axis=0)
    up_keyval = jnp.concatenate(exchanged(adapter_up_key_value), axis=0)

    segment_row = token_request_ids[0]
    my_holders = lax.dynamic_index_in_dim(slot_table, store, 0, keepdims=False) // per_store
    requests = jnp.arange(STORE_REQUESTS, dtype=jnp.int32)
    holder_order = (store - jnp.arange(stores, dtype=jnp.int32)) % stores
    served = jnp.max(
        jnp.where(my_holders[None, :] == holder_order[:, None], requests[None, :], -1), axis=1
    )
    members = (segment_row[:, None] == served[None, :]).astype(F32)
    starts = jnp.sum((segment_row[:, None] < requests[None, :]).astype(jnp.int32), axis=0)
    first_index = jnp.sum(
        jnp.where(segment_row[:, None] == requests[None, :], starts[None, :], 0), axis=1
    )
    positions = jnp.arange(total, dtype=jnp.int32) - first_index
    exponent = jnp.arange(HEAD_SIZE // 2, dtype=F32) * (2.0 / HEAD_SIZE)
    frequency = jnp.exp(-exponent * math.log(rope_theta))
    angles = positions.astype(F32)[:, None] * frequency[None, :]
    cosine, sine = jnp.cos(angles), jnp.sin(angles)
    cosine = jnp.concatenate([cosine, cosine], axis=1)
    sine = jnp.concatenate([-sine, sine], axis=1)
    holds_keys = z % 2 == 0
    key_cosine = jnp.where(holds_keys, cosine, 1.0)
    key_sine = jnp.where(holds_keys, sine, 0.0)

    def block_of(array, index):
        return lax.dynamic_slice_in_dim(array, jnp.clip(index, 0, n - 1) * rows, rows, 0)

    def every_chunk(way, k):
        return [way[k, c] for c in range(chunks)]

    parts = {}
    first = low_parts(
        [[tokens]], jnp.int32(0), z * width_share, width_share, downs, [block_of(members, z)]
    )
    low_sum = first
    for k in range(1, n):
        if k < half:
            both = low_parts(
                [every_chunk(down, k), every_chunk(up, k)],
                home_chunk,
                home_offset,
                width_share,
                downs,
                [block_of(members, z + k), block_of(members, z - k)],
            )
            low_sum = low_sum + lax.ppermute(
                both[:rows], "tensor", [(i, i + k) for i in range(n - k)]
            )
            low_sum = low_sum + lax.ppermute(
                both[rows:], "tensor", [(i, i - k) for i in range(k, n)]
            )
        else:
            one = low_parts(
                [
                    [down[k, c] for c in range(chunks // 2)]
                    + [up[k, c] for c in range(chunks // 2, chunks)]
                ],
                home_chunk,
                home_offset,
                width_share,
                downs,
                [block_of(members, jnp.where(side == 0, z + k, z - k))],
            )
            low_sum = low_sum + lax.ppermute(
                one,
                "tensor",
                [(i, i + k) for i in range(n - k)] + [(i, i - k) for i in range(k, n)],
            )
    low_own = low_sum.astype(BF16)
    low_turned = [low_own] + [
        lax.ppermute(low_own, "tensor", [((i + r) % n, i) for i in range(n)]) for r in range(1, n)
    ]
    low = lax.dynamic_slice_in_dim(
        jnp.concatenate(low_turned + low_turned, axis=0), (n - z) % n * rows, total, 0
    )

    weights = [query_weight, key_value_weight]
    sources = []
    own_q, own_kv = project(
        [[[down[0, c]]] for c in range(chunks)], [0], list(range(chunks)), weights
    )
    sources.append((own_q, own_kv, 0, lambda b, zz: b == zz))
    side_chunks = [jnp.where(side == 0, a, chunks - 1 - a) for a in range(chunks)]

    def sided(k, a):
        return [down[k, a], up[k, chunks - 1 - a]]

    for k in range(1, late):
        if k < half:
            q, kv = project(
                [[[down[k, c]], [up[k, c]]] for c in range(chunks)],
                [0, 0],
                list(range(chunks)),
                weights,
            )
            sources.append((q, kv, 0, lambda b, zz, k=k: b == zz + k))
            sources.append((q, kv, rows, lambda b, zz, k=k: b == zz - k))
        else:
            q, kv = project(
                [[sided(k, a)] for a in range(chunks)],
                jnp.stack([side]),
                jnp.stack(side_chunks),
                weights,
            )
            sources.append((q, kv, 0, lambda b, zz, k=k: (b == zz + k) | (b == zz - k)))
    late_q, late_kv = project(
        [[sided(late, a)] for a in range(chunks - 1)],
        jnp.stack([side]),
        jnp.stack(side_chunks[: chunks - 1]),
        weights,
    )

    group_size = QUERY_HEADS // KEY_VALUE_HEADS
    head_local = query_width // HEAD_SIZE
    pair_heads = keyval_width // HEAD_SIZE
    used = max(head_local // group_size, 1)

    def first_used(rank):
        return rank * head_local // group_size - rank // 2 * pair_heads

    partner = z ^ 1
    cuts = (first_used(z), first_used(partner), used)
    query, mine, send = finish(
        sources,
        z,
        low,
        members,
        up_query,
        up_keyval,
        (cosine, sine, key_cosine, key_sine),
        cuts,
        n,
    )
    recv = lax.ppermute(send, "tensor", [(i, i ^ 1) for i in range(n)])

    late_block = jnp.where(side == 0, n - 1, 0)
    late_args = dict(
        candidates=sided(late, chunks - 1), pick=side, chunk_id=side_chunks[chunks - 1]
    )
    late_low = block_of(low, late_block)
    late_member = block_of(members, late_block)
    mine_late, send_late = finish_late(
        **late_args,
        weight=key_value_weight,
        sums=late_kv,
        low=late_low[:, ADAPTER_RANK:],
        member=late_member,
        up=up_keyval,
        cosine=block_of(key_cosine, late_block),
        sine=block_of(key_sine, late_block),
        cuts=cuts,
    )
    recv_late = lax.ppermute(send_late, "tensor", [(0, 1), (n - 1, n - 2)])
    (query_late,) = finish_late(
        **late_args,
        weight=query_weight,
        sums=late_q,
        low=late_low[:, :ADAPTER_RANK],
        member=late_member,
        up=up_query,
        cosine=block_of(cosine, late_block),
        sine=block_of(sine, late_block),
    )
    nowhere = jnp.int32(-1)
    own_late = jnp.where(z == 0, (n - 1) * rows, jnp.where(z == n - 1, 0, nowhere))
    partner_late = jnp.where(partner == 0, (n - 1) * rows, jnp.where(partner == n - 1, 0, nowhere))
    info = jnp.stack([own_late, partner_late, holds_keys.astype(jnp.int32)]).astype(jnp.int32)
    return attend(
        query,
        query_late,
        mine,
        mine_late,
        recv,
        recv_late,
        segment_row[:, None],
        segment_row[None, :],
        info,
        n,
    )


def solution(mesh):
    return jax.shard_map(
        on_device,
        mesh=mesh,
        in_specs=(
            P(("groups", "store", "tensor"), None),
            P(None, "tensor"),
            P(None, "tensor"),
            P("store", None, "tensor"),
            P("store", None, "tensor"),
            P("store", None, "tensor"),
            P("groups"),
            P("groups", None),
            P(("groups", "store"), None),
        ),
        out_specs=P(("groups", "store"), "tensor"),
        check_vma=False,
    )
```

```python
import functools
import math

import jax
import jax.numpy as jnp
from jax import lax
from jax.experimental import pallas as pl
from jax.experimental.pallas import tpu as pltpu
from jax.sharding import PartitionSpec as P

QUERY_HEADS = 64
KEY_VALUE_HEADS = 8
HEAD_SIZE = 128
ADAPTER_RANK = 64
STORE_REQUESTS = 4
LONGEST_REQUEST = 256

adapter_scale = 2.0
rope_theta = 500000.0

CHUNKS = 4
TILE = 128
VMEM_LIMIT = 40 * 2**20
F32 = jnp.float32
BF16 = jnp.bfloat16
ANY = pl.BlockSpec(memory_space=pltpu.HBM)


def after(arrays, *others):
    return lax.optimization_barrier((arrays, others))[0]


def params():
    return pltpu.CompilerParams(vmem_limit_bytes=VMEM_LIMIT)


def whole(shape):
    return pl.BlockSpec(shape, lambda *_: (0,) * len(shape))


def start_picked(candidates, pick, target, semaphore, columns=None):
    def start(source):
        view = source if columns is None else source.at[:, columns]
        pltpu.make_async_copy(view, target, semaphore).start()

    if len(candidates) == 1:
        start(candidates[0])
        return
    for index, source in enumerate(candidates):
        pl.when(pick == index)(functools.partial(start, source))


def project(candidates, picks, chunk_ids, weights, starts=None):
    steps, groups = len(candidates), len(candidates[0])
    rows, chunk = candidates[0][0][0].shape
    block = min(1024, chunk)
    sub = chunk // block
    flat = [x for at_chunk in candidates for group in at_chunk for x in group]
    widths = [w.shape[1] for w in weights]
    count = len(weights)

    def kernel(info, *refs):
        tokens_in = iter(refs[: len(flat)])
        sources = [[[next(tokens_in) for _ in group] for group in at_chunk] for at_chunk in candidates]
        rest = refs[len(flat) :]
        weight_refs, rest = rest[:count], rest[count:]
        start_refs = ()
        if starts is not None:
            start_refs, rest = rest[:count], rest[count:]
        out_refs, (held, sems) = rest[:count], rest[count:]
        step = pl.program_id(0)
        at = step // sub

        @pl.when(step == 0)
        def _():
            for a in range(steps):
                for r in range(groups):
                    start_picked(
                        sources[a][r], info[r], held.at[a, pl.ds(r * rows, rows), :], sems.at[a, r]
                    )

        @pl.when(step % sub == 0)
        def _():
            for r in range(groups):
                pltpu.make_async_copy(
                    sources[0][r][0], held.at[at, pl.ds(r * rows, rows), :], sems.at[at, r]
                ).wait()

        part = held[at, :, pl.ds(pl.multiple_of((step % sub) * block, block), block)]
        for i in range(count):
            product = jnp.dot(part, weight_refs[i][...], preferred_element_type=F32)

            @pl.when(step == 0)
            def _(i=i, product=product):
                out_refs[i][...] = product if starts is None else start_refs[i][...] + product

            @pl.when(step > 0)
            def _(i=i, product=product):
                out_refs[i][...] += product

    height = groups * rows
    info = jnp.concatenate([jnp.asarray(picks, jnp.int32), jnp.asarray(chunk_ids, jnp.int32)])
    results = pl.pallas_call(
        kernel,
        grid_spec=pltpu.PrefetchScalarGridSpec(
            num_scalar_prefetch=1,
            grid=(steps * sub,),
            in_specs=[ANY] * len(flat)
            + [
                pl.BlockSpec(
                    (block, w), lambda g, info: (info[groups + g // sub] * sub + g % sub, 0)
                )
                for w in widths
            ]
            + ([whole((height, w)) for w in widths] if starts is not None else []),
            out_specs=[whole((height, w)) for w in widths],
            scratch_shapes=[
                pltpu.VMEM((steps, height, chunk), BF16),
                pltpu.SemaphoreType.DMA((steps, groups)),
            ],
        ),
        out_shape=[jax.ShapeDtypeStruct((height, w), F32) for w in widths],
        compiler_params=params(),
        cost_estimate=pl.CostEstimate(
            flops=2 * height * steps * chunk * sum(widths),
            bytes_accessed=2 * steps * chunk * (sum(widths) + height),
            transcendentals=0,
        ),
    )(info, *flat, *weights, *(starts or []))
    return results


def low_parts(candidates, pick, offset, width, downs, member_groups):
    groups = len(candidates)
    rows = candidates[0][0].shape[0]
    flat = [x for group in candidates for x in group]
    holders = len(downs)
    rank = downs[0].shape[0]
    members = jnp.concatenate(member_groups, axis=0)

    def kernel(info, *refs):
        tokens_in = iter(refs[: len(flat)])
        sources = [[next(tokens_in) for _ in group] for group in candidates]
        down_refs = refs[len(flat) : len(flat) + holders]
        member_ref, out_ref, held, sems = refs[len(flat) + holders :]
        columns = pl.ds(pl.multiple_of(info[1], 128), width)
        for r in range(groups):
            start_picked(sources[r], info[0], held.at[pl.ds(r * rows, rows), :], sems.at[r], columns)
        for r in range(groups):
            pltpu.make_async_copy(
                sources[r][0].at[:, columns], held.at[pl.ds(r * rows, rows), :], sems.at[r]
            ).wait()
        total = None
        for d in range(holders):
            product = lax.dot_general(
                held[...], down_refs[d][...], (((1,), (1,)), ((), ())), preferred_element_type=F32
            )
            term = product * member_ref[:, d : d + 1]
            total = term if total is None else total + term
        out_ref[...] = total

    return pl.pallas_call(
        kernel,
        grid_spec=pltpu.PrefetchScalarGridSpec(
            num_scalar_prefetch=1,
            grid=(1,),
            in_specs=[ANY] * len(flat)
            + [whole(d.shape) for d in downs]
            + [whole(members.shape)],
            out_specs=whole((groups * rows, rank)),
            scratch_shapes=[
                pltpu.VMEM((groups * rows, width), BF16),
                pltpu.SemaphoreType.DMA((groups,)),
            ],
        ),
        out_shape=jax.ShapeDtypeStruct((groups * rows, rank), F32),
        compiler_params=params(),
        cost_estimate=pl.CostEstimate(
            flops=2 * groups * rows * width * rank * holders,
            bytes_accessed=2 * width * (groups * rows + rank * holders),
            transcendentals=0,
        ),
    )(jnp.stack([pick, offset]).astype(jnp.int32), *flat, *downs, members)


def spread(low, member):
    return jnp.concatenate([low * member[:, d : d + 1] for d in range(member.shape[1])], axis=1)


def rotate(block, cosine, sine):
    return block * cosine + pltpu.roll(block, HEAD_SIZE // 2, 1) * sine


def finish(sources, rank_index, low, members, up_query, up_keyval, tables, firsts, blocks):
    rows = low.shape[0] // blocks
    query_width = up_query.shape[1]
    keyval_width = up_keyval.shape[1]
    used = firsts[2] * HEAD_SIZE
    rank = ADAPTER_RANK
    count = len(sources)

    def kernel(info, *refs):
        sums = refs[: 2 * count]
        (low_ref, member_ref, upq_ref, upkv_ref, cos_ref, sin_ref, kcos_ref, ksin_ref) = refs[
            2 * count : 2 * count + 8
        ]
        query_ref, mine_ref, send_ref, held_q, held_kv, sems = refs[2 * count + 8 :]
        block = pl.program_id(0)
        z = info[0]
        for i, (_, _, first, test) in enumerate(sources):

            @pl.when(test(block, z))
            def _(i=i, first=first):
                a = pltpu.make_async_copy(sums[2 * i].at[pl.ds(first, rows), :], held_q, sems.at[0])
                b = pltpu.make_async_copy(
                    sums[2 * i + 1].at[pl.ds(first, rows), :], held_kv, sems.at[1]
                )
                a.start()
                b.start()
                a.wait()
                b.wait()

        member = member_ref[...].astype(BF16)
        low_block = low_ref[...]
        update = jnp.dot(
            spread(low_block[:, :rank], member), upq_ref[...], preferred_element_type=F32
        )
        for h in range(query_width // HEAD_SIZE):
            at = slice(h * HEAD_SIZE, (h + 1) * HEAD_SIZE)
            query_ref[:, at] = rotate(
                held_q[:, at] + adapter_scale * update[:, at], cos_ref[...], sin_ref[...]
            ).astype(BF16)
        update = jnp.dot(
            spread(low_block[:, rank:], member), upkv_ref[...], preferred_element_type=F32
        )
        for h in range(keyval_width // HEAD_SIZE):
            at = slice(h * HEAD_SIZE, (h + 1) * HEAD_SIZE)
            held_kv[:, at] = rotate(
                held_kv[:, at] + adapter_scale * update[:, at], kcos_ref[...], ksin_ref[...]
            )
        mine_ref[...] = held_kv[:, pl.ds(pl.multiple_of(info[1], HEAD_SIZE), used)].astype(BF16)
        send_ref[...] = held_kv[:, pl.ds(pl.multiple_of(info[2], HEAD_SIZE), used)].astype(BF16)

    def by_block(width):
        return pl.BlockSpec((rows, width), lambda b, info: (b, 0))

    flat = [x for q, kv, _, _ in sources for x in (q, kv)]
    total = rows * blocks
    info = jnp.stack([rank_index, firsts[0] * HEAD_SIZE, firsts[1] * HEAD_SIZE]).astype(jnp.int32)
    return pl.pallas_call(
        kernel,
        grid_spec=pltpu.PrefetchScalarGridSpec(
            num_scalar_prefetch=1,
            grid=(blocks,),
            in_specs=[ANY] * len(flat)
            + [
                by_block(low.shape[1]),
                by_block(members.shape[1]),
                whole(up_query.shape),
                whole(up_keyval.shape),
            ]
            + [by_block(HEAD_SIZE)] * 4,
            out_specs=[by_block(query_width), by_block(used), by_block(used)],
            scratch_shapes=[
                pltpu.VMEM((rows, query_width), F32),
                pltpu.VMEM((rows, keyval_width), F32),
                pltpu.SemaphoreType.DMA((2,)),
            ],
        ),
        out_shape=[
            jax.ShapeDtypeStruct((total, query_width), BF16),
            jax.ShapeDtypeStruct((total, used), BF16),
            jax.ShapeDtypeStruct((total, used), BF16),
        ],
        compiler_params=params(),
        cost_estimate=pl.CostEstimate(
            flops=2 * total * up_query.shape[0] * (query_width + keyval_width),
            bytes_accessed=8 * total * (query_width + keyval_width),
            transcendentals=0,
        ),
    )(info, *flat, low, members, up_query, up_keyval, *tables)


def finish_late(candidates, pick, chunk_id, weight, sums, low, member, up, cosine, sine, cuts=None):
    rows, chunk = candidates[0].shape
    width = weight.shape[1]
    step_width = min(512, width)
    steps = width // step_width
    count = len(candidates)

    def kernel(info, *refs):
        sources = refs[:count]
        weight_ref, sum_ref, low_ref, member_ref, up_ref, cos_ref, sin_ref = refs[count : count + 7]
        rest = refs[count + 7 :]
        outs, (held, sem) = rest[:-2], rest[-2:]

        @pl.when(pl.program_id(0) == 0)
        def _():
            start_picked(sources, info[0], held, sem.at[0])
            pltpu.make_async_copy(sources[0], held, sem.at[0]).wait()

        update = jnp.dot(
            spread(low_ref[...], member_ref[...].astype(BF16)),
            up_ref[...],
            preferred_element_type=F32,
        )
        raw = (
            jnp.dot(held[...], weight_ref[...], preferred_element_type=F32)
            + sum_ref[...]
            + adapter_scale * update
        )
        parts = [
            rotate(raw[:, h * HEAD_SIZE : (h + 1) * HEAD_SIZE], cos_ref[...], sin_ref[...])
            for h in range(step_width // HEAD_SIZE)
        ]
        if cuts is None:
            for h, part in enumerate(parts):
                outs[0][:, h * HEAD_SIZE : (h + 1) * HEAD_SIZE] = part.astype(BF16)
        else:
            for out, first in ((outs[0], info[2]), (outs[1], info[3])):
                for u in range(cuts[2]):
                    chosen = parts[0]
                    for h in range(1, len(parts)):
                        chosen = jnp.where(first + u == h, parts[h], chosen)
                    out[:, u * HEAD_SIZE : (u + 1) * HEAD_SIZE] = chosen.astype(BF16)

    def column(height):
        return pl.BlockSpec((height, step_width), lambda g, info: (0, g))

    if cuts is None:
        outs = [jax.ShapeDtypeStruct((rows, width), BF16)]
        out_specs = [column(rows)]
        info = [pick, chunk_id]
    else:
        used = cuts[2] * HEAD_SIZE
        outs = [jax.ShapeDtypeStruct((rows, used), BF16)] * 2
        out_specs = [whole((rows, used))] * 2
        info = [pick, chunk_id, cuts[0], cuts[1]]
    return pl.pallas_call(
        kernel,
        grid_spec=pltpu.PrefetchScalarGridSpec(
            num_scalar_prefetch=1,
            grid=(steps,),
            in_specs=[ANY] * count
            + [
                pl.BlockSpec((chunk, step_width), lambda g, info: (info[1], g)),
                column(rows),
                whole(low.shape),
                whole(member.shape),
                column(up.shape[0]),
                whole(cosine.shape),
                whole(sine.shape),
            ],
            out_specs=out_specs,
            scratch_shapes=[pltpu.VMEM((rows, chunk), BF16), pltpu.SemaphoreType.DMA((1,))],
        ),
        out_shape=outs,
        compiler_params=params(),
        cost_estimate=pl.CostEstimate(
            flops=2 * rows * width * (chunk + up.shape[0]),
            bytes_accessed=2 * width * chunk,
            transcendentals=0,
        ),
    )(jnp.stack(info).astype(jnp.int32), *candidates, weight, sums, low, member, up, cosine, sine)


def attend(query, query_late, mine, mine_late, recv, recv_late, ids_column, ids_row, info, blocks):
    total, width = query.shape
    rows = total // blocks
    heads = width // HEAD_SIZE
    used = mine.shape[1] // HEAD_SIZE
    per_kv = heads // used
    together = min(4, per_kv)
    span = together * HEAD_SIZE
    scale = math.log2(math.e) / math.sqrt(HEAD_SIZE)
    tiles = total // TILE
    back = -(-(LONGEST_REQUEST - 1) // TILE)

    def kernel(info, q_ref, ql_ref, m_ref, ml_ref, r_ref, rl_ref, idc_ref, idr_ref, out_ref, k_ref, v_ref):
        step = pl.program_id(0)

        @pl.when(step == 0)
        def _():
            def put(keys_mine):
                own, other = (k_ref, v_ref) if keys_mine else (v_ref, k_ref)
                own[...] = m_ref[...]
                other[...] = r_ref[...]

                @pl.when(info[0] >= 0)
                def _():
                    own[pl.ds(pl.multiple_of(info[0], rows), rows), :] = ml_ref[...]

                @pl.when(info[1] >= 0)
                def _():
                    other[pl.ds(pl.multiple_of(info[1], rows), rows), :] = rl_ref[...]

            pl.when(info[2] == 1)(lambda: put(True))
            pl.when(info[2] == 0)(lambda: put(False))

        @pl.when(info[0] >= 0)
        def _():
            q_ref[pl.ds(pl.multiple_of(info[0], rows), rows), :] = ql_ref[...]

        kv_at = pl.ds(pl.multiple_of((step * together // per_kv) * HEAD_SIZE, HEAD_SIZE), HEAD_SIZE)
        for tile in range(tiles):
            low_tile = max(0, tile - back)
            key_rows = (tile + 1 - low_tile) * TILE
            at = slice(tile * TILE, (tile + 1) * TILE)
            keys = k_ref[low_tile * TILE : low_tile * TILE + key_rows, kv_at]
            values = v_ref[low_tile * TILE : low_tile * TILE + key_rows, kv_at]
            row_index = lax.broadcasted_iota(jnp.int32, (TILE, key_rows), 0) + tile * TILE
            column_index = lax.broadcasted_iota(jnp.int32, (TILE, key_rows), 1) + low_tile * TILE
            allowed = (idc_ref[at, :] == idr_ref[:, low_tile * TILE : low_tile * TILE + key_rows]) & (
                row_index >= column_index
            )
            for h in range(together):
                query_part = q_ref[at, h * HEAD_SIZE : (h + 1) * HEAD_SIZE]
                scores = lax.dot_general(
                    query_part, keys, (((1,), (1,)), ((), ())), preferred_element_type=F32
                )
                scores = jnp.where(allowed, scores * scale, -1e30)
                top = jnp.max(scores, axis=1, keepdims=True)
                weights = jnp.exp2(scores - top)
                norm = jnp.sum(weights, axis=1, keepdims=True)
                mixed = jnp.dot(weights.astype(BF16), values, preferred_element_type=F32)
                out_ref[at, h * HEAD_SIZE : (h + 1) * HEAD_SIZE] = (mixed * (1.0 / norm)).astype(BF16)

    by_heads = pl.BlockSpec((total, span), lambda g, info: (0, g))
    return pl.pallas_call(
        kernel,
        grid_spec=pltpu.PrefetchScalarGridSpec(
            num_scalar_prefetch=1,
            grid=(heads // together,),
            in_specs=[
                by_heads,
                pl.BlockSpec((rows, span), lambda g, info: (0, g)),
                whole(mine.shape),
                whole(mine_late.shape),
                whole(recv.shape),
                whole(recv_late.shape),
                whole(ids_column.shape),
                whole(ids_row.shape),
            ],
            out_specs=by_heads,
            scratch_shapes=[pltpu.VMEM(mine.shape, BF16), pltpu.VMEM(mine.shape, BF16)],
        ),
        out_shape=jax.ShapeDtypeStruct((total, width), BF16),
        compiler_params=params(),
        cost_estimate=pl.CostEstimate(
            flops=4 * total * total * width,
            bytes_accessed=4 * total * width,
            transcendentals=total * total * heads,
        ),
    )(info, query, query_late, mine, mine_late, recv, recv_late, ids_column, ids_row)


def on_device(
    tokens,
    query_weight,
    key_value_weight,
    adapter_down_maps,
    adapter_up_query,
    adapter_up_key_value,
    adapter_row_table,
    request_adapter_ids,
    token_request_ids,
):
    z = lax.axis_index("tensor")
    store = lax.axis_index("store")
    n = lax.axis_size("tensor")
    stores = lax.axis_size("store")
    rows, model_width = tokens.shape
    total = rows * n
    half = n // 2
    late = n - 1
    chunks = CHUNKS
    chunk_width = model_width // chunks
    width_share = model_width // n
    slices = n // chunks
    home_chunk = z // slices
    home_offset = (z % slices) * width_share
    side = (z >= half).astype(jnp.int32)
    query_width = query_weight.shape[1]
    keyval_width = key_value_weight.shape[1]

    down = {(0, c): tokens[:, c * chunk_width : (c + 1) * chunk_width] for c in range(chunks)}
    up = dict(down)
    ahead = [(k, 0) for k in range(1, n)]
    behind = [(k, a) for k in range(1, n) for a in range(1, chunks)]
    turns = [t for both in zip(ahead, behind) for t in both] + behind[len(ahead) :]
    def send_turn(i, *others):
        k, a = turns[i]
        b = chunks - 1 - a
        if i >= 2:
            k_before, a_before = turns[i - 2]
            others += (down[k_before, a_before], up[k_before, chunks - 1 - a_before])
        send_down, send_up = after((down[k - 1, a], up[k - 1, b]), *others)
        down[k, a] = lax.ppermute(send_down, "tensor", [(j, j - 1) for j in range(1, n - k + 1)])
        up[k, b] = lax.ppermute(send_up, "tensor", [(j, j + 1) for j in range(k - 1, n - 1)])

    def turn_of(k):
        return max(i for i, (j, _) in enumerate(turns) if j == k)

    send_turn(0)
    send_turn(1)

    per_store = adapter_down_maps.shape[0]
    lookup = (
        request_adapter_ids[:, :, None]
        == jnp.arange(adapter_row_table.shape[0], dtype=jnp.int32)[None, None, :]
    ).astype(jnp.int32)
    slot_table = jnp.sum(lookup * adapter_row_table[None, None, :], axis=2)
    here = slot_table // per_store == store
    local = jnp.sum(jnp.where(here, slot_table - store * per_store, 0), axis=1)

    stacks = [adapter_down_maps, adapter_up_key_value, adapter_up_query]
    got = [[], [], []]
    last = down[0, 0]
    sent = []
    for which, stack in enumerate(stacks):
        for d in range(stores):
            target = (store + d) % stores
            row = lax.dynamic_index_in_dim(local, target, 0, keepdims=False)
            part = lax.dynamic_index_in_dim(stack, row, 0, keepdims=False)
            if d:
                part = after(part, last)
                sent.append(part)
                last = part = lax.ppermute(
                    part, "store", [(i, (i + d) % stores) for i in range(stores)]
                )
            got[which].append(part)
    downs, up_keyval, up_query = got
    up_query = jnp.concatenate(up_query, axis=0)
    up_keyval = jnp.concatenate(up_keyval, axis=0)

    segment_row = token_request_ids[0]
    my_holders = lax.dynamic_index_in_dim(slot_table, store, 0, keepdims=False) // per_store
    requests = jnp.arange(STORE_REQUESTS, dtype=jnp.int32)
    holder_order = (store - jnp.arange(stores, dtype=jnp.int32)) % stores
    served = jnp.max(
        jnp.where(my_holders[None, :] == holder_order[:, None], requests[None, :], -1), axis=1
    )
    members = (segment_row[:, None] == served[None, :]).astype(F32)
    starts = jnp.sum((segment_row[:, None] < requests[None, :]).astype(jnp.int32), axis=0)
    first_index = jnp.sum(
        jnp.where(segment_row[:, None] == requests[None, :], starts[None, :], 0), axis=1
    )
    positions = jnp.arange(total, dtype=jnp.int32) - first_index
    exponent = jnp.arange(HEAD_SIZE // 2, dtype=F32) * (2.0 / HEAD_SIZE)
    frequency = jnp.exp(-exponent * math.log(rope_theta))
    angles = positions.astype(F32)[:, None] * frequency[None, :]
    cosine, sine = jnp.cos(angles), jnp.sin(angles)
    cosine = jnp.concatenate([cosine, cosine], axis=1)
    sine = jnp.concatenate([-sine, sine], axis=1)
    holds_keys = z % 2 == 0
    key_cosine = jnp.where(holds_keys, cosine, 1.0)
    key_sine = jnp.where(holds_keys, sine, 0.0)

    def block_of(array, index):
        return lax.dynamic_slice_in_dim(array, jnp.clip(index, 0, n - 1) * rows, rows, 0)

    def every_chunk(way, k):
        return [way[k, c] for c in range(chunks)]

    weights = [query_weight, key_value_weight]
    sources = []
    own_q, own_kv = project(
        [[[down[0, c]]] for c in range(chunks)],
        after(jnp.zeros((1,), jnp.int32), downs[0], sent[0]),
        list(range(chunks)),
        weights,
    )
    sources.append((own_q, own_kv, 0, lambda b, zz: b == zz))
    side_chunks = [jnp.where(side == 0, a, chunks - 1 - a) for a in range(chunks)]

    def sided(k, a):
        return [down[k, a], up[k, chunks - 1 - a]]

    hold = {2: own_kv}
    next_turn = 2

    def send_until(turn):
        nonlocal next_turn
        while next_turn <= min(turn, len(turns) - 1):
            send_turn(next_turn, *([hold[next_turn]] if next_turn in hold else []))
            next_turn += 1

    def near(k):
        return [
            ([down[k, c] for c in range(chunks)], z + k),
            ([up[k, c] for c in range(chunks)], z - k),
        ]

    def far(k):
        return (
            [down[k, c] for c in range(chunks // 2)] + [up[k, c] for c in range(chunks // 2, chunks)],
            jnp.where(side == 0, z + k, z - k),
        )

    def low_of(groups):
        return low_parts(
            [g for g, _ in groups],
            home_chunk,
            home_offset,
            width_share,
            downs,
            [block_of(members, b) for _, b in groups],
        )

    low_sum = low_parts(
        [[tokens]], jnp.int32(0), z * width_share, width_share, downs, [block_of(members, z)]
    )
    projected = {}
    for k in range(1, half):
        send_until(turn_of(k) + 2)
        both = low_of(near(k))
        low_sum = low_sum + lax.ppermute(both[:rows], "tensor", [(i, i + k) for i in range(n - k)])
        low_sum = low_sum + lax.ppermute(both[rows:], "tensor", [(i, i - k) for i in range(k, n)])
        q, kv = project(
            [[[down[k, c]], [up[k, c]]] for c in range(chunks)],
            after(jnp.zeros((2,), jnp.int32), both),
            list(range(chunks)),
            weights,
        )
        hold[turn_of(k) + 3] = kv
        sources.append((q, kv, 0, lambda b, zz, k=k: b == zz + k))
        sources.append((q, kv, rows, lambda b, zz, k=k: b == zz - k))
    far_home = max(i for i, (_, a) in enumerate(turns) if a < chunks // 2)
    send_until(far_home)
    far_low = low_of([far(k) for k in range(half, n)])
    for k in range(half, n):
        low_sum = low_sum + lax.ppermute(
            far_low[(k - half) * rows : (k - half + 1) * rows],
            "tensor",
            [(i, i + k) for i in range(n - k)] + [(i, i - k) for i in range(k, n)],
        )
    low_own = low_sum.astype(BF16)
    low_turned = [low_own] + [
        lax.ppermute(low_own, "tensor", [((i + r) % n, i) for i in range(n)]) for r in range(1, n)
    ]
    low = lax.dynamic_slice_in_dim(
        jnp.concatenate(low_turned + low_turned, axis=0), (n - z) % n * rows, total, 0
    )

    for k in range(half, late):
        send_until(turn_of(k) + 2)
        q, kv = project(
            [[sided(k, a)] for a in range(chunks)],
            after(jnp.stack([side]), low),
            jnp.stack(side_chunks),
            weights,
        )
        hold[turn_of(k) + 3] = kv
        sources.append((q, kv, 0, lambda b, zz, k=k: (b == zz + k) | (b == zz - k)))
    send_until(len(turns))
    group_size = QUERY_HEADS // KEY_VALUE_HEADS
    head_local = query_width // HEAD_SIZE
    pair_heads = keyval_width // HEAD_SIZE
    used = max(head_local // group_size, 1)

    def first_used(rank):
        return rank * head_local // group_size - rank // 2 * pair_heads

    partner = z ^ 1
    cuts = (first_used(z), first_used(partner), used)
    query, mine, send = finish(
        sources,
        z,
        low,
        members,
        up_query,
        up_keyval,
        (cosine, sine, key_cosine, key_sine),
        cuts,
        n,
    )
    recv = lax.ppermute(send, "tensor", [(i, i ^ 1) for i in range(n)])
    late_q, late_kv = project(
        [[sided(late, a)] for a in range(chunks - 1)],
        after(jnp.stack([side]), mine),
        jnp.stack(side_chunks[: chunks - 1]),
        weights,
    )

    late_block = jnp.where(side == 0, n - 1, 0)
    late_args = dict(
        candidates=sided(late, chunks - 1), pick=side, chunk_id=side_chunks[chunks - 1]
    )
    late_low = block_of(low, late_block)
    late_member = block_of(members, late_block)
    mine_late, send_late = finish_late(
        **late_args,
        weight=key_value_weight,
        sums=late_kv,
        low=late_low[:, ADAPTER_RANK:],
        member=late_member,
        up=up_keyval,
        cosine=block_of(key_cosine, late_block),
        sine=block_of(key_sine, late_block),
        cuts=cuts,
    )
    recv_late = lax.ppermute(send_late, "tensor", [(0, 1), (n - 1, n - 2)])
    (query_late,) = finish_late(
        **late_args,
        weight=query_weight,
        sums=late_q,
        low=late_low[:, :ADAPTER_RANK],
        member=late_member,
        up=up_query,
        cosine=block_of(cosine, late_block),
        sine=block_of(sine, late_block),
    )
    nowhere = jnp.int32(-1)
    own_late = jnp.where(z == 0, (n - 1) * rows, jnp.where(z == n - 1, 0, nowhere))
    partner_late = jnp.where(partner == 0, (n - 1) * rows, jnp.where(partner == n - 1, 0, nowhere))
    info = jnp.stack([own_late, partner_late, holds_keys.astype(jnp.int32)]).astype(jnp.int32)
    return attend(
        query,
        query_late,
        mine,
        mine_late,
        recv,
        recv_late,
        segment_row[:, None],
        segment_row[None, :],
        info,
        n,
    )


def solution(mesh):
    return jax.shard_map(
        on_device,
        mesh=mesh,
        in_specs=(
            P(("groups", "store", "tensor"), None),
            P(None, "tensor"),
            P(None, "tensor"),
            P("store", None, "tensor"),
            P("store", None, "tensor"),
            P("store", None, "tensor"),
            P("groups"),
            P("groups", None),
            P(("groups", "store"), None),
        ),
        out_specs=P(("groups", "store"), "tensor"),
        check_vma=False,
    )
```

```python
import functools
import math

import jax
import jax.numpy as jnp
from jax import lax
from jax.experimental import pallas as pl
from jax.experimental.pallas import tpu as pltpu
from jax.sharding import PartitionSpec as P

QUERY_HEADS = 64
KEY_VALUE_HEADS = 8
HEAD_SIZE = 128
ADAPTER_RANK = 64
STORE_REQUESTS = 4
LONGEST_REQUEST = 256

adapter_scale = 2.0
rope_theta = 500000.0

CHUNKS = 4
TILE = 128
MIB = 2**20
F32 = jnp.float32
BF16 = jnp.bfloat16
ANY = pl.BlockSpec(memory_space=pl.ANY)


def after(arrays, *others):
    return lax.optimization_barrier((arrays, others))[0]


def params(held):
    return pltpu.CompilerParams(vmem_limit_bytes=max(int(held) + 8 * MIB, 58 * MIB))


def whole(shape):
    return pl.BlockSpec(shape, lambda *_: (0,) * len(shape))


def unique(arrays):
    kept, places = [], []
    for x in arrays:
        at = next((i for i, y in enumerate(kept) if y is x), len(kept))
        if at == len(kept):
            kept.append(x)
        places.append(at)
    return kept, places


def start_picked(candidates, pick, width, target, semaphore):
    def start(source, first):
        pltpu.make_async_copy(source.at[:, pl.ds(first, width)], target, semaphore).start()

    if len(candidates) == 1:
        start(*candidates[0])
        return
    for index, (source, first) in enumerate(candidates):
        pl.when(pick == index)(functools.partial(start, source, first))


def pack(down_maps, up_query, up_keyval, local):
    stores = local.shape[0]
    _, down_rows, width = down_maps.shape
    _, rank, keyval_width = up_keyval.shape
    cut = width // keyval_width
    strip = rank // cut

    def kernel(rows, down_ref, upq_ref, upkv_ref, *rest):
        outs, sems = rest[:stores], rest[stores]
        copies = []
        for d in range(stores):
            out = outs[d]
            copies.append((down_ref.at[rows[d]], out.at[pl.ds(0, down_rows), :]))
            copies.append((upq_ref.at[rows[d]], out.at[pl.ds(down_rows, rank), :]))
            for i in range(cut):
                copies.append(
                    (
                        upkv_ref.at[rows[d], pl.ds(i * strip, strip), :],
                        out.at[
                            pl.ds(down_rows + rank, strip), pl.ds(i * keyval_width, keyval_width)
                        ],
                    )
                )
        copies = [
            pltpu.make_async_copy(source, target, sems.at[i])
            for i, (source, target) in enumerate(copies)
        ]
        for copy in copies:
            copy.start()
        for copy in copies:
            copy.wait()

    return pl.pallas_call(
        kernel,
        grid_spec=pltpu.PrefetchScalarGridSpec(
            num_scalar_prefetch=1,
            grid=(1,),
            in_specs=[ANY] * 3,
            out_specs=[ANY] * stores,
            scratch_shapes=[pltpu.SemaphoreType.DMA((stores * (2 + cut),))],
        ),
        out_shape=[jax.ShapeDtypeStruct((down_rows + rank + strip, width), BF16)] * stores,
        compiler_params=params(0),
    )(local, down_maps, up_query, up_keyval)


def project(candidates, picks, chunk_ids, chunk, weights):
    steps, groups = len(candidates), len(candidates[0])
    rows = candidates[0][0][0][0].shape[0]
    block = min(1024, chunk)
    sub = chunk // block
    arrays, places = unique([x for a in candidates for group in a for x, _ in group])
    widths = [w.shape[1] for w in weights]
    count = len(weights)

    def kernel(info, *refs):
        place = iter(places)
        sources = [[[(refs[next(place)], c) for _, c in group] for group in a] for a in candidates]
        rest = refs[len(arrays) :]
        weight_refs, out_refs, (held, sems) = rest[:count], rest[count : 2 * count], rest[2 * count :]
        step = pl.program_id(0)
        at = step // sub

        @pl.when(step == 0)
        def _():
            for a in range(steps):
                for r in range(groups):
                    target = held.at[a, pl.ds(r * rows, rows), :]
                    start_picked(sources[a][r], info[r], chunk, target, sems.at[a, r])

        @pl.when(step % sub == 0)
        def _():
            for r in range(groups):
                pltpu.make_async_copy(
                    sources[0][r][0][0].at[:, pl.ds(0, chunk)],
                    held.at[at, pl.ds(r * rows, rows), :],
                    sems.at[at, r],
                ).wait()

        part = held[at, :, pl.ds(pl.multiple_of((step % sub) * block, block), block)]
        for i in range(count):
            product = jnp.dot(part, weight_refs[i][...], preferred_element_type=F32)

            @pl.when(step == 0)
            def _(i=i, product=product):
                out_refs[i][...] = product

            @pl.when(step > 0)
            def _(i=i, product=product):
                out_refs[i][...] += product

    height = groups * rows
    info = jnp.concatenate([jnp.asarray(picks, jnp.int32), jnp.asarray(chunk_ids, jnp.int32)])
    return pl.pallas_call(
        kernel,
        grid_spec=pltpu.PrefetchScalarGridSpec(
            num_scalar_prefetch=1,
            grid=(steps * sub,),
            in_specs=[ANY] * len(arrays)
            + [
                pl.BlockSpec(
                    (block, w), lambda g, info: (info[groups + g // sub] * sub + g % sub, 0)
                )
                for w in widths
            ],
            out_specs=[whole((height, w)) for w in widths],
            scratch_shapes=[
                pltpu.VMEM((steps, height, chunk), BF16),
                pltpu.SemaphoreType.DMA((steps, groups)),
            ],
        ),
        out_shape=[jax.ShapeDtypeStruct((height, w), F32) for w in widths],
        compiler_params=params(
            2 * steps * height * chunk + (4 * block + 8 * height) * sum(widths)
        ),
        cost_estimate=pl.CostEstimate(
            flops=2 * height * steps * chunk * sum(widths),
            bytes_accessed=2 * steps * chunk * (sum(widths) + height),
            transcendentals=0,
        ),
    )(info, *arrays, *weights)


def low_parts(slots, pick, width, packed, members):
    arrays, places = unique([x for group, _, _ in slots for x, _ in group])
    count, holders = len(slots), len(packed)
    rows = arrays[0].shape[0]
    total = members.shape[0]
    rank = 2 * ADAPTER_RANK
    firsts = jnp.stack([jnp.asarray(c, jnp.int32) for group, _, _ in slots for _, c in group])
    info = jnp.concatenate(
        [
            jnp.stack([pick]),
            jnp.stack([b for _, b, _ in slots]),
            jnp.stack([v.astype(jnp.int32) for _, _, v in slots]),
            firsts,
        ]
    ).astype(jnp.int32)

    def kernel(info, *refs):
        place = iter(enumerate(places))
        sources = []
        for group, _, _ in slots:
            at = [next(place) for _ in group]
            sources.append(
                [(refs[p], pl.multiple_of(info[1 + 2 * count + i], HEAD_SIZE)) for i, p in at]
            )
        pack_refs = refs[len(arrays) : len(arrays) + holders]
        member_ref, out_ref, held, sems = refs[len(arrays) + holders :]
        for i in range(count):
            pl.when(info[1 + count + i] == 1)(
                functools.partial(
                    start_picked, sources[i], info[0], width, held.at[i], sems.at[i]
                )
            )
        for i in range(count):

            @pl.when(info[1 + count + i] == 1)
            def _(i=i):
                pltpu.make_async_copy(
                    sources[i][0][0].at[:, pl.ds(0, width)], held.at[i], sems.at[i]
                ).wait()
                here = pl.ds(pl.multiple_of(info[1 + i] * rows, rows), rows)
                member = member_ref[here, :]
                sum_ = None
                for d in range(holders):
                    product = lax.dot_general(
                        held[i],
                        pack_refs[d][:rank, :],
                        (((1,), (1,)), ((), ())),
                        preferred_element_type=F32,
                    )
                    term = product * member[:, d : d + 1]
                    sum_ = term if sum_ is None else sum_ + term
                out_ref[here, :] = sum_

    return pl.pallas_call(
        kernel,
        grid_spec=pltpu.PrefetchScalarGridSpec(
            num_scalar_prefetch=1,
            grid=(1,),
            in_specs=[ANY] * len(arrays)
            + [whole(p.shape) for p in packed]
            + [whole(members.shape)],
            out_specs=whole((total, rank)),
            scratch_shapes=[
                pltpu.VMEM((count, rows, width), BF16),
                pltpu.SemaphoreType.DMA((count,)),
            ],
        ),
        out_shape=jax.ShapeDtypeStruct((total, rank), F32),
        compiler_params=params(
            2 * count * rows * width
            + 4 * holders * packed[0].size
            + 16 * total * HEAD_SIZE
        ),
        cost_estimate=pl.CostEstimate(
            flops=2 * total * width * rank * holders,
            bytes_accessed=2 * width * (total + rank * holders),
            transcendentals=0,
        ),
    )(info, *arrays, *packed, members)


def spread(low, member):
    return jnp.concatenate([low * member[:, d : d + 1] for d in range(member.shape[1])], axis=1)


def rotate(block, cosine, sine):
    return block * cosine + pltpu.roll(block, HEAD_SIZE // 2, 1) * sine


def finish(sources, rank_index, low, members, packed, tables, firsts, blocks):
    rows = low.shape[0] // blocks
    query_width = sources[0][0].shape[1]
    keyval_width = sources[0][1].shape[1]
    used = firsts[2] * HEAD_SIZE
    rank = ADAPTER_RANK
    count = len(sources)
    holders = len(packed)
    cut = query_width // keyval_width
    strip = rank // cut
    sums_in, places = unique([x for q, kv, _, _ in sources for x in (q, kv)])

    def kernel(info, *refs):
        sums = [refs[p] for p in places]
        rest = refs[len(sums_in) :]
        pack_refs, rest = rest[:holders], rest[holders:]
        low_ref, member_ref, cos_ref, sin_ref, kcos_ref, ksin_ref = rest[:6]
        query_ref, mine_ref, send_ref, upq_ref, upkv_ref, held_q, held_kv, sems = rest[6:]
        block = pl.program_id(0)
        z = info[0]

        @pl.when(block == 0)
        def _():
            for d, packed_ref in enumerate(pack_refs):
                at = d * rank
                upq_ref[at : at + rank, :] = packed_ref[2 * rank : 3 * rank, :]
                for i in range(cut):
                    upkv_ref[at + i * strip : at + (i + 1) * strip, :] = packed_ref[
                        3 * rank : 3 * rank + strip, i * keyval_width : (i + 1) * keyval_width
                    ]

        for i, (_, _, first, test) in enumerate(sources):

            @pl.when(test(block, z))
            def _(i=i, first=first):
                a = pltpu.make_async_copy(sums[2 * i].at[pl.ds(first, rows), :], held_q, sems.at[0])
                b = pltpu.make_async_copy(
                    sums[2 * i + 1].at[pl.ds(first, rows), :], held_kv, sems.at[1]
                )
                a.start()
                b.start()
                a.wait()
                b.wait()

        member = member_ref[...].astype(BF16)
        low_block = low_ref[...]
        update = jnp.dot(
            spread(low_block[:, :rank], member), upq_ref[...], preferred_element_type=F32
        )
        for h in range(query_width // HEAD_SIZE):
            at = slice(h * HEAD_SIZE, (h + 1) * HEAD_SIZE)
            query_ref[:, at] = rotate(
                held_q[:, at] + adapter_scale * update[:, at], cos_ref[...], sin_ref[...]
            ).astype(BF16)
        update = jnp.dot(
            spread(low_block[:, rank:], member), upkv_ref[...], preferred_element_type=F32
        )
        for h in range(keyval_width // HEAD_SIZE):
            at = slice(h * HEAD_SIZE, (h + 1) * HEAD_SIZE)
            held_kv[:, at] = rotate(
                held_kv[:, at] + adapter_scale * update[:, at], kcos_ref[...], ksin_ref[...]
            )
        mine_ref[...] = held_kv[:, pl.ds(pl.multiple_of(info[1], HEAD_SIZE), used)].astype(BF16)
        send_ref[...] = held_kv[:, pl.ds(pl.multiple_of(info[2], HEAD_SIZE), used)].astype(BF16)

    def by_block(width):
        return pl.BlockSpec((rows, width), lambda b, info: (b, 0))

    total = rows * blocks
    info = jnp.stack([rank_index, firsts[0] * HEAD_SIZE, firsts[1] * HEAD_SIZE]).astype(jnp.int32)
    return pl.pallas_call(
        kernel,
        grid_spec=pltpu.PrefetchScalarGridSpec(
            num_scalar_prefetch=1,
            grid=(blocks,),
            in_specs=[ANY] * len(sums_in)
            + [whole(p.shape) for p in packed]
            + [by_block(low.shape[1]), by_block(members.shape[1])]
            + [by_block(HEAD_SIZE)] * 4,
            out_specs=[
                by_block(query_width),
                by_block(used),
                by_block(used),
                whole((holders * rank, query_width)),
                whole((holders * rank, keyval_width)),
            ],
            scratch_shapes=[
                pltpu.VMEM((rows, query_width), F32),
                pltpu.VMEM((rows, keyval_width), F32),
                pltpu.SemaphoreType.DMA((2,)),
            ],
        ),
        out_shape=[
            jax.ShapeDtypeStruct((total, query_width), BF16),
            jax.ShapeDtypeStruct((total, used), BF16),
            jax.ShapeDtypeStruct((total, used), BF16),
            jax.ShapeDtypeStruct((holders * rank, query_width), BF16),
            jax.ShapeDtypeStruct((holders * rank, keyval_width), BF16),
        ],
        compiler_params=params(
            4 * holders * packed[0].size
            + (12 * rows + 4 * holders * rank) * (query_width + keyval_width)
        ),
        cost_estimate=pl.CostEstimate(
            flops=2 * total * holders * rank * (query_width + keyval_width),
            bytes_accessed=8 * total * (query_width + keyval_width),
            transcendentals=0,
        ),
    )(info, *sums_in, *packed, low, members, *tables)


def finish_late(candidates, pick, chunk_id, weight, sums, low, member, up, cosine, sine, cuts=None):
    rows = candidates[0][0].shape[0]
    chunk = weight.shape[0] // CHUNKS
    width = weight.shape[1]
    step_width = min(512, width)
    steps = width // step_width
    count = len(candidates)

    def kernel(info, *refs):
        sources = [(ref, c) for ref, (_, c) in zip(refs, candidates)]
        weight_ref, sum_ref, low_ref, member_ref, up_ref, cos_ref, sin_ref = refs[count : count + 7]
        rest = refs[count + 7 :]
        outs, (held, sem) = rest[:-2], rest[-2:]

        @pl.when(pl.program_id(0) == 0)
        def _():
            start_picked(sources, info[0], chunk, held, sem.at[0])
            pltpu.make_async_copy(
                sources[0][0].at[:, pl.ds(0, chunk)], held, sem.at[0]
            ).wait()

        update = jnp.dot(
            spread(low_ref[...], member_ref[...].astype(BF16)),
            up_ref[...],
            preferred_element_type=F32,
        )
        raw = (
            jnp.dot(held[...], weight_ref[...], preferred_element_type=F32)
            + sum_ref[...]
            + adapter_scale * update
        )
        parts = [
            rotate(raw[:, h * HEAD_SIZE : (h + 1) * HEAD_SIZE], cos_ref[...], sin_ref[...])
            for h in range(step_width // HEAD_SIZE)
        ]
        if cuts is None:
            for h, part in enumerate(parts):
                outs[0][:, h * HEAD_SIZE : (h + 1) * HEAD_SIZE] = part.astype(BF16)
        else:
            for out, first in ((outs[0], info[2]), (outs[1], info[3])):
                for u in range(cuts[2]):
                    chosen = parts[0]
                    for h in range(1, len(parts)):
                        chosen = jnp.where(first + u == h, parts[h], chosen)
                    out[:, u * HEAD_SIZE : (u + 1) * HEAD_SIZE] = chosen.astype(BF16)

    def column(height):
        return pl.BlockSpec((height, step_width), lambda g, info: (0, g))

    if cuts is None:
        outs = [jax.ShapeDtypeStruct((rows, width), BF16)]
        out_specs = [column(rows)]
        info = [pick, chunk_id]
    else:
        used = cuts[2] * HEAD_SIZE
        outs = [jax.ShapeDtypeStruct((rows, used), BF16)] * 2
        out_specs = [whole((rows, used))] * 2
        info = [pick, chunk_id, cuts[0], cuts[1]]
    return pl.pallas_call(
        kernel,
        grid_spec=pltpu.PrefetchScalarGridSpec(
            num_scalar_prefetch=1,
            grid=(steps,),
            in_specs=[ANY] * count
            + [
                pl.BlockSpec((chunk, step_width), lambda g, info: (info[1], g)),
                column(rows),
                whole(low.shape),
                whole(member.shape),
                column(up.shape[0]),
                whole(cosine.shape),
                whole(sine.shape),
            ],
            out_specs=out_specs,
            scratch_shapes=[pltpu.VMEM((rows, chunk), BF16), pltpu.SemaphoreType.DMA((1,))],
        ),
        out_shape=outs,
        compiler_params=params(4 * (chunk + up.shape[0] + 4 * rows) * step_width + 2 * rows * chunk),
        cost_estimate=pl.CostEstimate(
            flops=2 * rows * width * (chunk + up.shape[0]),
            bytes_accessed=2 * width * chunk,
            transcendentals=0,
        ),
    )(jnp.stack(info).astype(jnp.int32), *[x for x, _ in candidates], weight, sums, low, member, up, cosine, sine)


def attend(query, query_late, mine, mine_late, recv, recv_late, ids_column, ids_row, info, blocks):
    total, width = query.shape
    rows = total // blocks
    heads = width // HEAD_SIZE
    used = mine.shape[1] // HEAD_SIZE
    per_kv = heads // used
    together = min(4, per_kv)
    span = together * HEAD_SIZE
    scale = math.log2(math.e) / math.sqrt(HEAD_SIZE)
    tiles = total // TILE
    back = -(-(LONGEST_REQUEST - 1) // TILE)

    def kernel(info, q_ref, ql_ref, m_ref, ml_ref, r_ref, rl_ref, idc_ref, idr_ref, out_ref, k_ref, v_ref):
        step = pl.program_id(0)

        @pl.when(step == 0)
        def _():
            def put(keys_mine):
                own, other = (k_ref, v_ref) if keys_mine else (v_ref, k_ref)
                own[...] = m_ref[...]
                other[...] = r_ref[...]

                @pl.when(info[0] >= 0)
                def _():
                    own[pl.ds(pl.multiple_of(info[0], rows), rows), :] = ml_ref[...]

                @pl.when(info[1] >= 0)
                def _():
                    other[pl.ds(pl.multiple_of(info[1], rows), rows), :] = rl_ref[...]

            pl.when(info[2] == 1)(lambda: put(True))
            pl.when(info[2] == 0)(lambda: put(False))

        @pl.when(info[0] >= 0)
        def _():
            q_ref[pl.ds(pl.multiple_of(info[0], rows), rows), :] = ql_ref[...]

        kv_at = pl.ds(pl.multiple_of((step * together // per_kv) * HEAD_SIZE, HEAD_SIZE), HEAD_SIZE)
        for tile in range(tiles):
            low_tile = max(0, tile - back)
            key_rows = (tile + 1 - low_tile) * TILE
            at = slice(tile * TILE, (tile + 1) * TILE)
            keys = k_ref[low_tile * TILE : low_tile * TILE + key_rows, kv_at]
            values = v_ref[low_tile * TILE : low_tile * TILE + key_rows, kv_at]
            row_index = lax.broadcasted_iota(jnp.int32, (TILE, key_rows), 0) + tile * TILE
            column_index = lax.broadcasted_iota(jnp.int32, (TILE, key_rows), 1) + low_tile * TILE
            allowed = (idc_ref[at, :] == idr_ref[:, low_tile * TILE : low_tile * TILE + key_rows]) & (
                row_index >= column_index
            )
            for h in range(together):
                query_part = q_ref[at, h * HEAD_SIZE : (h + 1) * HEAD_SIZE]
                scores = lax.dot_general(
                    query_part, keys, (((1,), (1,)), ((), ())), preferred_element_type=F32
                )
                scores = jnp.where(allowed, scores * scale, -1e30)
                top = jnp.max(scores, axis=1, keepdims=True)
                weights = jnp.exp2(scores - top)
                norm = jnp.sum(weights, axis=1, keepdims=True)
                mixed = jnp.dot(weights.astype(BF16), values, preferred_element_type=F32)
                out_ref[at, h * HEAD_SIZE : (h + 1) * HEAD_SIZE] = (mixed * (1.0 / norm)).astype(BF16)

    by_heads = pl.BlockSpec((total, span), lambda g, info: (0, g))
    return pl.pallas_call(
        kernel,
        grid_spec=pltpu.PrefetchScalarGridSpec(
            num_scalar_prefetch=1,
            grid=(heads // together,),
            in_specs=[
                by_heads,
                pl.BlockSpec((rows, span), lambda g, info: (0, g)),
                whole(mine.shape),
                whole(mine_late.shape),
                whole(recv.shape),
                whole(recv_late.shape),
                whole(ids_column.shape),
                whole(ids_row.shape),
            ],
            out_specs=by_heads,
            scratch_shapes=[pltpu.VMEM(mine.shape, BF16), pltpu.VMEM(mine.shape, BF16)],
        ),
        out_shape=jax.ShapeDtypeStruct((total, width), BF16),
        compiler_params=params(8 * total * span + 12 * mine.size + 4 * MIB),
        cost_estimate=pl.CostEstimate(
            flops=4 * total * total * width,
            bytes_accessed=4 * total * width,
            transcendentals=total * total * heads,
        ),
    )(info, query, query_late, mine, mine_late, recv, recv_late, ids_column, ids_row)


def on_device(
    tokens,
    query_weight,
    key_value_weight,
    adapter_down_maps,
    adapter_up_query,
    adapter_up_key_value,
    adapter_row_table,
    request_adapter_ids,
    token_request_ids,
):
    z = lax.axis_index("tensor")
    store = lax.axis_index("store")
    n = lax.axis_size("tensor")
    stores = lax.axis_size("store")
    rows, model_width = tokens.shape
    total = rows * n
    half = n // 2
    late = n - 1
    chunks = CHUNKS
    chunk_width = model_width // chunks
    width_share = model_width // n
    slices = n // chunks
    home_chunk = z // slices
    home_offset = (z % slices) * width_share
    side = (z >= half).astype(jnp.int32)
    query_width = query_weight.shape[1]
    keyval_width = key_value_weight.shape[1]

    front, back = (0, 1), (1, chunks)
    late_pieces = [front, (1, chunks - 1), (chunks - 1, chunks)]
    turns = [(k, piece) for k in range(1, late) for piece in (front, back)]
    turns += [(late, piece) for piece in late_pieces]
    down = {(0, (0, chunks)): tokens}
    up = dict(down)

    def mirrored(piece):
        return (chunks - piece[1], chunks - piece[0])

    def piece_at(way, k, chunk):
        for (j, (first, end)), x in way.items():
            if j == k and first <= chunk < end:
                return x, (chunk - first) * chunk_width

    def cut_out(way, k, piece):
        x, first = piece_at(way, k, piece[0])
        wide = (piece[1] - piece[0]) * chunk_width
        return x if x.shape[1] == wide else x[:, first : first + wide]

    came = {}

    def send_turn(i, *others):
        k, piece = turns[i]
        other_piece = mirrored(piece)
        if i >= 2:
            others += came[i - 2]
        sends = (cut_out(down, k - 1, piece), cut_out(up, k - 1, other_piece))
        if k == late:
            send = after(jnp.where(side == 0, *sends), *others)
            last_out[piece] = send
            came[i] = (lax.ppermute(send, "tensor", [(1, 0), (n - 2, n - 1)]),)
            last_in[piece] = came[i][0]
            return
        if i == 0:
            first_sends.extend(sends)
        if i == 1:
            others += tuple(first_sends)
        send_down, send_up = after(sends, *others)
        if i == 1:
            first_sends.extend((send_down, send_up))
        down[k, piece] = lax.ppermute(
            send_down, "tensor", [(j, j - 1) for j in range(1, n - k + 1)]
        )
        up[k, other_piece] = lax.ppermute(
            send_up, "tensor", [(j, j + 1) for j in range(k - 1, n - 1)]
        )
        came[i] = (down[k, piece], up[k, other_piece])

    def turn_of(k):
        return max(i for i, (j, _) in enumerate(turns) if j == k)

    hold = {}
    first_sends = []
    last_in, last_out = {}, {}
    next_turn = 0

    def send_until(turn):
        nonlocal next_turn
        while next_turn <= min(turn, len(turns) - 1):
            send_turn(next_turn, *([hold[next_turn]] if next_turn in hold else []))
            next_turn += 1

    send_until(1)

    per_store = adapter_down_maps.shape[0]
    lookup = (
        request_adapter_ids[:, :, None]
        == jnp.arange(adapter_row_table.shape[0], dtype=jnp.int32)[None, None, :]
    ).astype(jnp.int32)
    slot_table = jnp.sum(lookup * adapter_row_table[None, None, :], axis=2)
    here = slot_table // per_store == store
    local = jnp.sum(jnp.where(here, slot_table - store * per_store, 0), axis=1)

    packed = pack(
        adapter_down_maps,
        adapter_up_query,
        adapter_up_key_value,
        after(
            lax.dynamic_slice_in_dim(jnp.concatenate([local, local]), store, stores, 0), *first_sends
        ),
    )
    packed = list(packed)
    for d in range(1, stores):
        packed[d] = lax.ppermute(
            after(packed[d], packed[d - 1]), "store", [(i, (i + d) % stores) for i in range(stores)]
        )

    segment_row = token_request_ids[0]
    my_holders = lax.dynamic_index_in_dim(slot_table, store, 0, keepdims=False) // per_store
    requests = jnp.arange(STORE_REQUESTS, dtype=jnp.int32)
    holder_order = (store - jnp.arange(stores, dtype=jnp.int32)) % stores
    served = jnp.max(
        jnp.where(my_holders[None, :] == holder_order[:, None], requests[None, :], -1), axis=1
    )
    members = (segment_row[:, None] == served[None, :]).astype(F32)
    starts = jnp.sum((segment_row[:, None] < requests[None, :]).astype(jnp.int32), axis=0)
    first_index = jnp.sum(
        jnp.where(segment_row[:, None] == requests[None, :], starts[None, :], 0), axis=1
    )
    positions = jnp.arange(total, dtype=jnp.int32) - first_index
    exponent = jnp.arange(HEAD_SIZE // 2, dtype=F32) * (2.0 / HEAD_SIZE)
    frequency = jnp.exp(-exponent * math.log(rope_theta))
    angles = positions.astype(F32)[:, None] * frequency[None, :]
    cosine, sine = jnp.cos(angles), jnp.sin(angles)
    cosine = jnp.concatenate([cosine, cosine], axis=1)
    sine = jnp.concatenate([-sine, sine], axis=1)
    holds_keys = z % 2 == 0
    key_cosine = jnp.where(holds_keys, cosine, 1.0)
    key_sine = jnp.where(holds_keys, sine, 0.0)

    def block_of(array, index):
        return lax.dynamic_slice_in_dim(array, jnp.clip(index, 0, n - 1) * rows, rows, 0)

    weights = [query_weight, key_value_weight]
    sources = []
    side_chunks = [jnp.where(side == 0, a, chunks - 1 - a) for a in range(chunks)]

    def sided(k, a):
        return [piece_at(down, k, a), piece_at(up, k, chunks - 1 - a)]

    for k in range(1, half):
        send_until(turn_of(k) + 2)
        ways = ([(down, 0)] if k == 1 else []) + [(down, k), (up, k)]
        q, kv = project(
            [[[piece_at(way, j, c)] for way, j in ways] for c in range(chunks)],
            after(jnp.zeros((len(ways),), jnp.int32), *came[turn_of(k) + 1]),
            list(range(chunks)),
            chunk_width,
            weights,
        )
        hold[turn_of(k) + 4] = kv
        first = 0
        if k == 1:
            sources.append((q, kv, 0, lambda b, zz: b == zz))
            first = rows
        sources.append((q, kv, first, lambda b, zz, k=k: b == zz + k))
        sources.append((q, kv, first + rows, lambda b, zz, k=k: b == zz - k))
    for k in range(half, late):
        send_until(turn_of(k) + 2)
        q, kv = project(
            [[sided(k, a)] for a in range(chunks)],
            jnp.stack([side]),
            jnp.stack(side_chunks),
            chunk_width,
            weights,
        )
        hold[turn_of(k) + 3] = kv
        sources.append((q, kv, 0, lambda b, zz, k=k: (b == zz + k) | (b == zz - k)))
    send_until(len(turns))

    def home(way, k, c):
        x, first = piece_at(way, k, c)
        return x, first + home_offset

    slots = [([(tokens, z * width_share)], z, z >= 0)]
    for k in range(1, half):
        slots.append(([home(down, k, c) for c in range(chunks)], z + k, z + k < n))
        slots.append(([home(up, k, c) for c in range(chunks)], z - k, z >= k))
    for k in range(half, late):
        from_both = [home(down, k, c) for c in range(chunks // 2)]
        from_both += [home(up, k, c) for c in range(chunks // 2, chunks)]
        slots.append((from_both, jnp.where(side == 0, z + k, z - k), (z + k < n) | (z >= k)))
    front_in, middle_in, back_in = (last_in[piece] for piece in late_pieces)
    slots.append(([(front_in, home_offset)], jnp.where(side == 0, late, 0), (z == 0) | (z == late)))
    low_part = low_parts(
        slots, after(home_chunk, last_out[late_pieces[1]]), width_share, packed, members
    )
    low = lax.psum(low_part, "tensor").astype(BF16)

    group_size = QUERY_HEADS // KEY_VALUE_HEADS
    head_local = query_width // HEAD_SIZE
    pair_heads = keyval_width // HEAD_SIZE
    used = max(head_local // group_size, 1)

    def first_used(rank):
        return rank * head_local // group_size - rank // 2 * pair_heads

    partner = z ^ 1
    cuts = (first_used(z), first_used(partner), used)
    query, mine, send, up_query, up_keyval = finish(
        sources,
        z,
        low,
        members,
        packed,
        (cosine, sine, key_cosine, key_sine),
        cuts,
        n,
    )
    recv = lax.ppermute(send, "tensor", [(i, i ^ 1) for i in range(n)])
    late_q, late_kv = project(
        [[[(front_in, 0)]]] + [[[(middle_in, a * chunk_width)]] for a in range(chunks - 2)],
        after(jnp.zeros((1,), jnp.int32), low_part),
        jnp.stack([side_chunks[0]] + list(range(1, chunks - 1))),
        chunk_width,
        weights,
    )

    late_block = jnp.where(side == 0, n - 1, 0)
    late_args = dict(
        candidates=[(back_in, 0)], pick=side, chunk_id=side_chunks[chunks - 1]
    )
    late_low = block_of(low, late_block)
    late_member = block_of(members, late_block)
    mine_late, send_late = finish_late(
        **late_args,
        weight=key_value_weight,
        sums=late_kv,
        low=late_low[:, ADAPTER_RANK:],
        member=late_member,
        up=up_keyval,
        cosine=block_of(key_cosine, late_block),
        sine=block_of(key_sine, late_block),
        cuts=cuts,
    )
    recv_late = lax.ppermute(send_late, "tensor", [(0, 1), (n - 1, n - 2)])
    (query_late,) = finish_late(
        **late_args,
        weight=query_weight,
        sums=late_q,
        low=late_low[:, :ADAPTER_RANK],
        member=late_member,
        up=up_query,
        cosine=block_of(cosine, late_block),
        sine=block_of(sine, late_block),
    )
    nowhere = jnp.int32(-1)
    own_late = jnp.where(z == 0, (n - 1) * rows, jnp.where(z == n - 1, 0, nowhere))
    partner_late = jnp.where(partner == 0, (n - 1) * rows, jnp.where(partner == n - 1, 0, nowhere))
    info = jnp.stack([own_late, partner_late, holds_keys.astype(jnp.int32)]).astype(jnp.int32)
    return attend(
        query,
        query_late,
        mine,
        mine_late,
        recv,
        recv_late,
        segment_row[:, None],
        segment_row[None, :],
        info,
        n,
    )


def solution(mesh):
    return jax.shard_map(
        on_device,
        mesh=mesh,
        in_specs=(
            P(("groups", "store", "tensor"), None),
            P(None, "tensor"),
            P(None, "tensor"),
            P("store", None, "tensor"),
            P("store", None, "tensor"),
            P("store", None, "tensor"),
            P("groups"),
            P("groups", None),
            P(("groups", "store"), None),
        ),
        out_specs=P(("groups", "store"), "tensor"),
        check_vma=False,
    )
```

```python
import functools
import math

import jax
import jax.numpy as jnp
from jax import lax
from jax.experimental import pallas as pl
from jax.experimental.pallas import tpu as pltpu
from jax.sharding import PartitionSpec as P

QUERY_HEADS = 64
KEY_VALUE_HEADS = 8
HEAD_SIZE = 128
ADAPTER_RANK = 64
STORE_REQUESTS = 4
LONGEST_REQUEST = 256

adapter_scale = 2.0
rope_theta = 500000.0

CHUNKS = 4
TILE = 128
MIB = 2**20
F32 = jnp.float32
BF16 = jnp.bfloat16
ANY = pl.BlockSpec(memory_space=pl.ANY)


def after(arrays, *others):
    return lax.optimization_barrier((arrays, others))[0]


def params(held):
    return pltpu.CompilerParams(vmem_limit_bytes=max(int(held) + 8 * MIB, 58 * MIB))


def whole(shape):
    return pl.BlockSpec(shape, lambda *_: (0,) * len(shape))


def unique(arrays):
    kept, places = [], []
    for x in arrays:
        at = next((i for i, y in enumerate(kept) if y is x), len(kept))
        if at == len(kept):
            kept.append(x)
        places.append(at)
    return kept, places


def start_picked(candidates, pick, width, target, semaphore):
    def start(source, first):
        pltpu.make_async_copy(source.at[:, pl.ds(first, width)], target, semaphore).start()

    if len(candidates) == 1:
        start(*candidates[0])
        return
    for index, (source, first) in enumerate(candidates):
        pl.when(pick == index)(functools.partial(start, source, first))


def pack(down_maps, up_query, up_keyval, local):
    stores = local.shape[0]
    _, down_rows, width = down_maps.shape
    _, rank, keyval_width = up_keyval.shape
    cut = width // keyval_width
    strip = rank // cut

    height = down_rows + rank + strip

    def kernel(rows, down_ref, upq_ref, upkv_ref, *rest):
        outs, (held, sems, out_sems) = rest[:stores], rest[stores:]
        copies, writes = [], []
        for d in range(stores):
            here = held.at[d]
            sources = [
                (down_ref.at[rows[d]], here.at[pl.ds(0, down_rows), :]),
                (upq_ref.at[rows[d]], here.at[pl.ds(down_rows, rank), :]),
            ]
            for i in range(cut):
                sources.append(
                    (
                        upkv_ref.at[rows[d], pl.ds(i * strip, strip), :],
                        here.at[
                            pl.ds(down_rows + rank, strip), pl.ds(i * keyval_width, keyval_width)
                        ],
                    )
                )
            copies.append(
                [
                    pltpu.make_async_copy(source, target, sems.at[d, i])
                    for i, (source, target) in enumerate(sources)
                ]
            )
            writes.append(pltpu.make_async_copy(here, outs[d], out_sems.at[d]))
        for group in copies:
            for copy in group:
                copy.start()
        for group, write in zip(copies, writes):
            for copy in group:
                copy.wait()
            write.start()
        for write in writes:
            write.wait()

    return pl.pallas_call(
        kernel,
        grid_spec=pltpu.PrefetchScalarGridSpec(
            num_scalar_prefetch=1,
            grid=(1,),
            in_specs=[ANY] * 3,
            out_specs=[ANY] * stores,
            scratch_shapes=[
                pltpu.VMEM((stores, height, width), BF16),
                pltpu.SemaphoreType.DMA((stores, 2 + cut)),
                pltpu.SemaphoreType.DMA((stores,)),
            ],
        ),
        out_shape=[jax.ShapeDtypeStruct((height, width), BF16)] * stores,
        compiler_params=params(2 * stores * height * width),
    )(local, down_maps, up_query, up_keyval)


def project(candidates, picks, chunk_ids, chunk, weights, starts=None):
    steps, groups = len(candidates), len(candidates[0])
    rows = candidates[0][0][0][0].shape[0]
    block = min(1024, chunk)
    sub = chunk // block
    blocks = steps * sub
    ahead = min(3, blocks)
    arrays, places = unique([x for a in candidates for group in a for x, _ in group])
    widths = [w.shape[1] for w in weights]
    count = len(weights)
    height = groups * rows

    def kernel(info, *refs):
        place = iter(places)
        sources = [[[(refs[next(place)], c) for _, c in group] for group in a] for a in candidates]
        rest = refs[len(arrays) :]
        weight_refs, rest = rest[:count], rest[count:]
        if starts is not None:
            start_refs, rest = rest[:count], rest[count:]
        out_refs, rest = rest[:count], rest[count:]
        streams, (held, sems, stream_sems) = rest[:count], rest[count:]

        def loads(i, slot):
            at = info[groups + i // sub] * sub + i % sub
            here = pl.ds(pl.multiple_of(at * block, block), block)
            return [
                pltpu.make_async_copy(
                    weight_refs[w].at[here, :], streams[w].at[slot], stream_sems.at[slot, w]
                )
                for w in range(count)
            ]

        for a in range(steps):
            for r in range(groups):
                target = held.at[a, pl.ds(r * rows, rows), :]
                start_picked(sources[a][r], info[r], chunk, target, sems.at[a, r])
            if a == 0:
                for i in range(ahead):
                    for load in loads(i, i):
                        load.start()
        for w in range(count):
            out_refs[w][...] = jnp.zeros_like(out_refs[w]) if starts is None else start_refs[w][...]

        def body(i, carry):
            slot = lax.rem(i, ahead)
            at, part_at = i // sub, lax.rem(i, sub)

            @pl.when(part_at == 0)
            def _():
                for r in range(groups):
                    pltpu.make_async_copy(
                        sources[0][r][0][0].at[:, pl.ds(0, chunk)],
                        held.at[at, pl.ds(r * rows, rows), :],
                        sems.at[at, r],
                    ).wait()

            for load in loads(i, slot):
                load.wait()
            part = held[at, :, pl.ds(pl.multiple_of(part_at * block, block), block)]
            for w in range(count):
                out_refs[w][...] += jnp.dot(
                    part, streams[w][slot], preferred_element_type=F32
                )

            @pl.when(i + ahead < blocks)
            def _():
                for load in loads(i + ahead, slot):
                    load.start()

            return carry

        lax.fori_loop(0, blocks, body, 0)

    info = jnp.concatenate([jnp.asarray(picks, jnp.int32), jnp.asarray(chunk_ids, jnp.int32)])
    return pl.pallas_call(
        kernel,
        grid_spec=pltpu.PrefetchScalarGridSpec(
            num_scalar_prefetch=1,
            grid=(1,),
            in_specs=[ANY] * (len(arrays) + count)
            + ([whole((height, w)) for w in widths] if starts is not None else []),
            out_specs=[whole((height, w)) for w in widths],
            scratch_shapes=[pltpu.VMEM((ahead, block, w), BF16) for w in widths]
            + [
                pltpu.VMEM((steps, height, chunk), BF16),
                pltpu.SemaphoreType.DMA((steps, groups)),
                pltpu.SemaphoreType.DMA((ahead, count)),
            ],
        ),
        out_shape=[jax.ShapeDtypeStruct((height, w), F32) for w in widths],
        compiler_params=params(
            2 * steps * height * chunk + (2 * ahead * block + 16 * height) * sum(widths)
        ),
        cost_estimate=pl.CostEstimate(
            flops=2 * height * steps * chunk * sum(widths),
            bytes_accessed=2 * steps * chunk * (sum(widths) + height),
            transcendentals=0,
        ),
    )(info, *arrays, *weights, *(starts or []))


def low_parts(slots, pick, width, packed, members):
    arrays, places = unique([x for group, _, _ in slots for x, _ in group])
    count, holders = len(slots), len(packed)
    rows = arrays[0].shape[0]
    total = members.shape[0]
    rank = 2 * ADAPTER_RANK
    firsts = jnp.stack([jnp.asarray(c, jnp.int32) for group, _, _ in slots for _, c in group])
    info = jnp.concatenate(
        [
            jnp.stack([pick]),
            jnp.stack([b for _, b, _ in slots]),
            jnp.stack([v.astype(jnp.int32) for _, _, v in slots]),
            firsts,
        ]
    ).astype(jnp.int32)

    def kernel(info, *refs):
        place = iter(enumerate(places))
        sources = []
        for group, _, _ in slots:
            at = [next(place) for _ in group]
            sources.append(
                [(refs[p], pl.multiple_of(info[1 + 2 * count + i], HEAD_SIZE)) for i, p in at]
            )
        pack_refs = refs[len(arrays) : len(arrays) + holders]
        member_ref, out_ref, held, maps, sems, map_sems = refs[len(arrays) + holders :]
        loads = [
            pltpu.make_async_copy(
                pack_refs[d].at[pl.ds(0, rank), :],
                maps.at[pl.ds(d * rank, rank), :],
                map_sems.at[d],
            )
            for d in range(holders)
        ]
        for load in loads:
            load.start()
        for i in range(count):
            pl.when(info[1 + count + i] == 1)(
                functools.partial(
                    start_picked, sources[i], info[0], width, held.at[i], sems.at[i]
                )
            )
        for load in loads:
            load.wait()
        for i in range(count):

            @pl.when(info[1 + count + i] == 1)
            def _(i=i):
                pltpu.make_async_copy(
                    sources[i][0][0].at[:, pl.ds(0, width)], held.at[i], sems.at[i]
                ).wait()
                here = pl.ds(pl.multiple_of(info[1 + i] * rows, rows), rows)
                member = member_ref[here, :]
                product = lax.dot_general(
                    held[i], maps[...], (((1,), (1,)), ((), ())), preferred_element_type=F32
                )
                sum_ = product[:, :rank] * member[:, 0:1]
                for d in range(1, holders):
                    sum_ += product[:, d * rank : (d + 1) * rank] * member[:, d : d + 1]
                out_ref[here, :] = sum_.astype(BF16)

    return pl.pallas_call(
        kernel,
        grid_spec=pltpu.PrefetchScalarGridSpec(
            num_scalar_prefetch=1,
            grid=(1,),
            in_specs=[ANY] * (len(arrays) + holders) + [whole(members.shape)],
            out_specs=whole((total, rank)),
            scratch_shapes=[
                pltpu.VMEM((count, rows, width), BF16),
                pltpu.VMEM((holders * rank, width), BF16),
                pltpu.SemaphoreType.DMA((count,)),
                pltpu.SemaphoreType.DMA((holders,)),
            ],
        ),
        out_shape=jax.ShapeDtypeStruct((total, rank), BF16),
        compiler_params=params(
            2 * count * rows * width
            + 4 * holders * packed[0].size
            + 16 * total * HEAD_SIZE
        ),
        cost_estimate=pl.CostEstimate(
            flops=2 * total * width * rank * holders,
            bytes_accessed=2 * width * (total + rank * holders),
            transcendentals=0,
        ),
    )(info, *arrays, *packed, members)


def spread(low, member):
    return jnp.concatenate([low * member[:, d : d + 1] for d in range(member.shape[1])], axis=1)


def rotate(block, cosine, sine):
    return block * cosine + pltpu.roll(block, HEAD_SIZE // 2, 1) * sine


def finish(sources, rank_index, low, members, packed, tables, firsts, blocks):
    rows = low.shape[0] // blocks
    query_width = sources[0][0].shape[1]
    keyval_width = sources[0][1].shape[1]
    used = firsts[2] * HEAD_SIZE
    rank = ADAPTER_RANK
    count = len(sources)
    holders = len(packed)
    cut = query_width // keyval_width
    strip = rank // cut
    sums_in, places = unique([x for q, kv, _, _ in sources for x in (q, kv)])

    def kernel(info, *refs):
        sums = [refs[p] for p in places]
        rest = refs[len(sums_in) :]
        pack_refs, rest = rest[:holders], rest[holders:]
        low_ref, member_ref, cos_ref, sin_ref, kcos_ref, ksin_ref = rest[:6]
        query_ref, mine_ref, send_ref, upq_ref, upkv_ref = rest[6:11]
        held_q, held_kv, turned, sems, up_sems = rest[11:]
        block = pl.program_id(0)
        z = info[0]

        def loads(b, i):
            first = sources[i][2]
            return [
                pltpu.make_async_copy(
                    sums[2 * i + j].at[pl.ds(first, rows), :], held.at[b], sems.at[b, j]
                )
                for j, held in enumerate((held_q, held_kv))
            ]

        ups = []
        for d, packed_ref in enumerate(pack_refs):
            at = d * rank
            ups.append(
                (packed_ref.at[pl.ds(2 * rank, rank), :], upq_ref.at[pl.ds(at, rank), :])
            )
            for i in range(cut):
                ups.append(
                    (
                        packed_ref.at[
                            pl.ds(3 * rank, strip), pl.ds(i * keyval_width, keyval_width)
                        ],
                        upkv_ref.at[pl.ds(at + i * strip, strip), :],
                    )
                )
        ups = [pltpu.make_async_copy(a, b, up_sems.at[i]) for i, (a, b) in enumerate(ups)]

        @pl.when(block == 0)
        def _():
            for b in range(blocks):
                for i, (_, _, _, test) in enumerate(sources):

                    @pl.when(test(b, z))
                    def _(b=b, i=i):
                        for load in loads(b, i):
                            load.start()

            for load in ups:
                load.start()
            for load in ups:
                load.wait()

        def add_and_turn(b):
            member = member_ref[...].astype(BF16)
            low_block = low_ref[...]
            update = jnp.dot(
                spread(low_block[:, :rank], member), upq_ref[...], preferred_element_type=F32
            )
            for h in range(query_width // HEAD_SIZE):
                at = slice(h * HEAD_SIZE, (h + 1) * HEAD_SIZE)
                query_ref[:, at] = rotate(
                    held_q[b, :, at] + adapter_scale * update[:, at], cos_ref[...], sin_ref[...]
                ).astype(BF16)
            update = jnp.dot(
                spread(low_block[:, rank:], member), upkv_ref[...], preferred_element_type=F32
            )
            for h in range(keyval_width // HEAD_SIZE):
                at = slice(h * HEAD_SIZE, (h + 1) * HEAD_SIZE)
                turned[:, at] = rotate(
                    held_kv[b, :, at] + adapter_scale * update[:, at], kcos_ref[...], ksin_ref[...]
                )
            for out, first in ((mine_ref, info[1]), (send_ref, info[2])):
                out[...] = turned[:, pl.ds(pl.multiple_of(first, HEAD_SIZE), used)].astype(BF16)

        there = functools.reduce(jnp.logical_or, [test(block, z) for _, _, _, test in sources])

        @pl.when(there)
        def _():
            for load in loads(block, 0):
                load.wait()
            add_and_turn(block)

    def by_block(width):
        return pl.BlockSpec((rows, width), lambda b, info: (b, 0))

    total = rows * blocks
    info = jnp.stack([rank_index, firsts[0] * HEAD_SIZE, firsts[1] * HEAD_SIZE]).astype(jnp.int32)
    return pl.pallas_call(
        kernel,
        grid_spec=pltpu.PrefetchScalarGridSpec(
            num_scalar_prefetch=1,
            grid=(blocks,),
            in_specs=[ANY] * (len(sums_in) + holders)
            + [by_block(low.shape[1]), by_block(members.shape[1])]
            + [by_block(HEAD_SIZE)] * 4,
            out_specs=[
                by_block(query_width),
                by_block(used),
                by_block(used),
                whole((holders * rank, query_width)),
                whole((holders * rank, keyval_width)),
            ],
            scratch_shapes=[
                pltpu.VMEM((blocks, rows, query_width), F32),
                pltpu.VMEM((blocks, rows, keyval_width), F32),
                pltpu.VMEM((rows, keyval_width), F32),
                pltpu.SemaphoreType.DMA((blocks, 2)),
                pltpu.SemaphoreType.DMA((holders * (1 + cut),)),
            ],
        ),
        out_shape=[
            jax.ShapeDtypeStruct((total, query_width), BF16),
            jax.ShapeDtypeStruct((total, used), BF16),
            jax.ShapeDtypeStruct((total, used), BF16),
            jax.ShapeDtypeStruct((holders * rank, query_width), BF16),
            jax.ShapeDtypeStruct((holders * rank, keyval_width), BF16),
        ],
        compiler_params=params(
            (4 * total + 12 * rows + 4 * holders * rank) * (query_width + keyval_width)
        ),
        cost_estimate=pl.CostEstimate(
            flops=2 * total * holders * rank * (query_width + keyval_width),
            bytes_accessed=8 * total * (query_width + keyval_width),
            transcendentals=0,
        ),
    )(info, *sums_in, *packed, low, members, *tables)


def finish_late(piece, chunk_id, weight, sums, low, member, up, cosine, sine, cuts=None):
    rows, chunk = piece.shape
    width = weight.shape[1]
    step_width = min(1024, width)
    steps = width // step_width

    def kernel(info, x_ref, weight_ref, sum_ref, low_ref, member_ref, up_ref, cos_ref, sin_ref, *outs):
        update = jnp.dot(
            spread(low_ref[...], member_ref[...].astype(BF16)),
            up_ref[...],
            preferred_element_type=F32,
        )
        raw = (
            jnp.dot(x_ref[...], weight_ref[...], preferred_element_type=F32)
            + sum_ref[...]
            + adapter_scale * update
        )
        parts = [
            rotate(raw[:, h * HEAD_SIZE : (h + 1) * HEAD_SIZE], cos_ref[...], sin_ref[...])
            for h in range(step_width // HEAD_SIZE)
        ]
        if cuts is None:
            for h, part in enumerate(parts):
                outs[0][:, h * HEAD_SIZE : (h + 1) * HEAD_SIZE] = part.astype(BF16)
        else:
            for out, first in ((outs[0], info[1]), (outs[1], info[2])):
                for u in range(cuts[2]):
                    chosen = parts[0]
                    for h in range(1, len(parts)):
                        chosen = jnp.where(first + u == h, parts[h], chosen)
                    out[:, u * HEAD_SIZE : (u + 1) * HEAD_SIZE] = chosen.astype(BF16)

    def column(height):
        return pl.BlockSpec((height, step_width), lambda g, info: (0, g))

    if cuts is None:
        outs = [jax.ShapeDtypeStruct((rows, width), BF16)]
        out_specs = [column(rows)]
        info = [chunk_id]
    else:
        used = cuts[2] * HEAD_SIZE
        outs = [jax.ShapeDtypeStruct((rows, used), BF16)] * 2
        out_specs = [whole((rows, used))] * 2
        info = [chunk_id, cuts[0], cuts[1]]
    return pl.pallas_call(
        kernel,
        grid_spec=pltpu.PrefetchScalarGridSpec(
            num_scalar_prefetch=1,
            grid=(steps,),
            in_specs=[
                whole(piece.shape),
                pl.BlockSpec((chunk, step_width), lambda g, info: (info[0], g)),
                column(rows),
                whole(low.shape),
                whole(member.shape),
                column(up.shape[0]),
                whole(cosine.shape),
                whole(sine.shape),
            ],
            out_specs=out_specs,
        ),
        out_shape=outs,
        compiler_params=params(4 * (chunk + up.shape[0] + 4 * rows) * step_width + 4 * rows * chunk),
        cost_estimate=pl.CostEstimate(
            flops=2 * rows * width * (chunk + up.shape[0]),
            bytes_accessed=2 * width * chunk,
            transcendentals=0,
        ),
    )(jnp.stack(info).astype(jnp.int32), piece, weight, sums, low, member, up, cosine, sine)


def attend(query, query_late, mine, mine_late, recv, recv_late, ids_column, ids_row, info, blocks):
    total, width = query.shape
    rows = total // blocks
    heads = width // HEAD_SIZE
    used = mine.shape[1] // HEAD_SIZE
    per_kv = heads // used
    together = min(4, per_kv)
    span = together * HEAD_SIZE
    scale = math.log2(math.e) / math.sqrt(HEAD_SIZE)
    tiles = total // TILE
    back = -(-(LONGEST_REQUEST - 1) // TILE)

    longest = (back + 1) * TILE

    def kernel(info, q_ref, ql_ref, m_ref, ml_ref, r_ref, rl_ref, idc_ref, idr_ref, out_ref, *held):
        k_ref, v_ref, bias_ref, held_q = held
        step = pl.program_id(0)

        @pl.when(step == 0)
        def _():
            def put(keys_mine):
                own, other = (k_ref, v_ref) if keys_mine else (v_ref, k_ref)
                own[...] = m_ref[...]
                other[...] = r_ref[...]

                @pl.when(info[0] >= 0)
                def _():
                    own[pl.ds(pl.multiple_of(info[0], rows), rows), :] = ml_ref[...]

                @pl.when(info[1] >= 0)
                def _():
                    other[pl.ds(pl.multiple_of(info[1], rows), rows), :] = rl_ref[...]

            pl.when(info[2] == 1)(lambda: put(True))
            pl.when(info[2] == 0)(lambda: put(False))
            for tile in range(tiles):
                first = max(0, tile - back) * TILE
                size = (tile + 1) * TILE - first
                key_index = lax.broadcasted_iota(jnp.int32, (size, TILE), 0) + first
                row_index = lax.broadcasted_iota(jnp.int32, (size, TILE), 1) + tile * TILE
                same = idc_ref[first : first + size, :] == idr_ref[:, tile * TILE : (tile + 1) * TILE]
                bias_ref[tile, :size, :] = jnp.where(same & (row_index >= key_index), 0.0, -1e30)

        held_q[...] = q_ref[...]

        @pl.when(info[0] >= 0)
        def _():
            held_q[pl.ds(pl.multiple_of(info[0], rows), rows), :] = ql_ref[...]

        kv_at = pl.ds(pl.multiple_of((step * together // per_kv) * HEAD_SIZE, HEAD_SIZE), HEAD_SIZE)
        for tile in range(tiles):
            first = max(0, tile - back) * TILE
            size = (tile + 1) * TILE - first
            at = slice(tile * TILE, (tile + 1) * TILE)
            keys = k_ref[first : first + size, kv_at]
            values = v_ref[first : first + size, kv_at]
            values = jnp.concatenate([values, jnp.ones_like(values)], axis=1)
            for h in range(together):
                scores = lax.dot_general(
                    keys,
                    held_q[at, h * HEAD_SIZE : (h + 1) * HEAD_SIZE],
                    (((1,), (1,)), ((), ())),
                    preferred_element_type=F32,
                )
                scores = scores * scale + bias_ref[tile, :size, :]
                top = jnp.max(scores, axis=0, keepdims=True)
                weights = jnp.exp2(scores - top).astype(BF16)
                mixed = lax.dot_general(
                    weights, values, (((0,), (0,)), ((), ())), preferred_element_type=F32
                )
                out_ref[at, h * HEAD_SIZE : (h + 1) * HEAD_SIZE] = (
                    mixed[:, :HEAD_SIZE] / mixed[:, HEAD_SIZE:]
                ).astype(BF16)

    by_heads = pl.BlockSpec((total, span), lambda g, info: (0, g))
    return pl.pallas_call(
        kernel,
        grid_spec=pltpu.PrefetchScalarGridSpec(
            num_scalar_prefetch=1,
            grid=(heads // together,),
            in_specs=[
                by_heads,
                pl.BlockSpec((rows, span), lambda g, info: (0, g)),
                whole(mine.shape),
                whole(mine_late.shape),
                whole(recv.shape),
                whole(recv_late.shape),
                whole(ids_column.shape),
                whole(ids_row.shape),
            ],
            out_specs=by_heads,
            scratch_shapes=[
                pltpu.VMEM(mine.shape, BF16),
                pltpu.VMEM(mine.shape, BF16),
                pltpu.VMEM((tiles, longest, TILE), F32),
                pltpu.VMEM((total, span), BF16),
            ],
        ),
        out_shape=jax.ShapeDtypeStruct((total, width), BF16),
        compiler_params=params(8 * total * span + 12 * mine.size + 4 * MIB),
        cost_estimate=pl.CostEstimate(
            flops=4 * total * total * width,
            bytes_accessed=4 * total * width,
            transcendentals=total * total * heads,
        ),
    )(info, query, query_late, mine, mine_late, recv, recv_late, ids_column, ids_row)


def on_device(
    tokens,
    query_weight,
    key_value_weight,
    adapter_down_maps,
    adapter_up_query,
    adapter_up_key_value,
    adapter_row_table,
    request_adapter_ids,
    token_request_ids,
):
    z = lax.axis_index("tensor")
    store = lax.axis_index("store")
    n = lax.axis_size("tensor")
    stores = lax.axis_size("store")
    rows, model_width = tokens.shape
    total = rows * n
    half = n // 2
    late = n - 1
    chunks = CHUNKS
    chunk_width = model_width // chunks
    width_share = model_width // n
    slices = n // chunks
    home_chunk = z // slices
    home_offset = (z % slices) * width_share
    side = (z >= half).astype(jnp.int32)
    query_width = query_weight.shape[1]
    keyval_width = key_value_weight.shape[1]

    front, middle, rear = (0, 1), (1, chunks - 1), (chunks - 1, chunks)
    turns = [(k, piece) for k in range(1, n) for piece in (front, middle, rear)]
    at = turns.index((late, front))
    turns[at - 1], turns[at] = turns[at], turns[at - 1]
    place = {turn: i for i, turn in enumerate(turns)}
    down = {(0, (0, chunks)): tokens}
    up = dict(down)

    def mirrored(piece):
        return (chunks - piece[1], chunks - piece[0])

    def piece_at(way, k, chunk):
        for (j, (first, end)), x in way.items():
            if j == k and first <= chunk < end:
                return x, (chunk - first) * chunk_width

    def cut_out(way, k, piece):
        x, first = piece_at(way, k, piece[0])
        wide = (piece[1] - piece[0]) * chunk_width
        return x if x.shape[1] == wide else x[:, first : first + wide]

    came = {}

    def send_turn(i, *others):
        k, piece = turns[i]
        other_piece = mirrored(piece)
        if i >= 2:
            others += came[i - 2]
        sends = (cut_out(down, k - 1, piece), cut_out(up, k - 1, other_piece))
        if k == late:
            send = after(jnp.where(side == 0, *sends), *others)
            last_out[piece] = send
            came[i] = (lax.ppermute(send, "tensor", [(1, 0), (n - 2, n - 1)]),)
            last_in[piece] = came[i][0]
            return
        if i == 0:
            first_sends.extend(sends)
        if i == 1:
            others += tuple(first_sends)
        send_down, send_up = after(sends, *others)
        if i == 1:
            first_sends.extend((send_down, send_up))
        down[k, piece] = lax.ppermute(
            send_down, "tensor", [(j, j - 1) for j in range(1, n - k + 1)]
        )
        up[k, other_piece] = lax.ppermute(
            send_up, "tensor", [(j, j + 1) for j in range(k - 1, n - 1)]
        )
        came[i] = (down[k, piece], up[k, other_piece])

    hold = {}
    first_sends = []
    last_in, last_out = {}, {}
    next_turn = 0

    def send_until(turn):
        nonlocal next_turn
        while next_turn <= min(turn, len(turns) - 1):
            send_turn(next_turn, *([hold[next_turn]] if next_turn in hold else []))
            next_turn += 1

    send_until(1)

    per_store = adapter_down_maps.shape[0]
    lookup = (
        request_adapter_ids[:, :, None]
        == jnp.arange(adapter_row_table.shape[0], dtype=jnp.int32)[None, None, :]
    ).astype(jnp.int32)
    slot_table = jnp.sum(lookup * adapter_row_table[None, None, :], axis=2)
    here = slot_table // per_store == store
    local = jnp.sum(jnp.where(here, slot_table - store * per_store, 0), axis=1)

    packed = pack(
        adapter_down_maps,
        adapter_up_query,
        adapter_up_key_value,
        after(
            lax.dynamic_slice_in_dim(jnp.concatenate([local, local]), store, stores, 0), *first_sends
        ),
    )
    packed = list(packed)
    for d in range(1, stores):
        packed[d] = lax.ppermute(
            after(packed[d], packed[d - 1]), "store", [(i, (i + d) % stores) for i in range(stores)]
        )

    segment_row = token_request_ids[0]
    my_holders = lax.dynamic_index_in_dim(slot_table, store, 0, keepdims=False) // per_store
    requests = jnp.arange(STORE_REQUESTS, dtype=jnp.int32)
    holder_order = (store - jnp.arange(stores, dtype=jnp.int32)) % stores
    served = jnp.max(
        jnp.where(my_holders[None, :] == holder_order[:, None], requests[None, :], -1), axis=1
    )
    members = (segment_row[:, None] == served[None, :]).astype(F32)
    starts = jnp.sum((segment_row[:, None] < requests[None, :]).astype(jnp.int32), axis=0)
    first_index = jnp.sum(
        jnp.where(segment_row[:, None] == requests[None, :], starts[None, :], 0), axis=1
    )
    positions = jnp.arange(total, dtype=jnp.int32) - first_index
    exponent = jnp.arange(HEAD_SIZE // 2, dtype=F32) * (2.0 / HEAD_SIZE)
    frequency = jnp.exp(-exponent * math.log(rope_theta))
    angles = positions.astype(F32)[:, None] * frequency[None, :]
    cosine, sine = jnp.cos(angles), jnp.sin(angles)
    cosine = jnp.concatenate([cosine, cosine], axis=1)
    sine = jnp.concatenate([-sine, sine], axis=1)
    holds_keys = z % 2 == 0
    key_cosine = jnp.where(holds_keys, cosine, 1.0)
    key_sine = jnp.where(holds_keys, sine, 0.0)

    def block_of(array, index):
        return lax.dynamic_slice_in_dim(array, jnp.clip(index, 0, n - 1) * rows, rows, 0)

    weights = [query_weight, key_value_weight]
    sources = []
    side_chunks = [jnp.where(side == 0, a, chunks - 1 - a) for a in range(chunks)]

    def sided(k, a):
        return [piece_at(down, k, a), piece_at(up, k, chunks - 1 - a)]

    for k in range(1, half):
        send_until(place[k, rear] + 2)
        ways = ([(down, 0)] if k == 1 else []) + [(down, k), (up, k)]
        q, kv = project(
            [[[piece_at(way, j, c)] for way, j in ways] for c in range(chunks)],
            jnp.zeros((len(ways),), jnp.int32),
            list(range(chunks)),
            chunk_width,
            weights,
        )
        hold[place[k + 1, front] + 2] = kv
        first = 0
        if k == 1:
            sources.append((q, kv, 0, lambda b, zz: b == zz))
            first = rows
        sources.append((q, kv, first, lambda b, zz, k=k: b == zz + k))
        sources.append((q, kv, first + rows, lambda b, zz, k=k: b == zz - k))

    def far_block(k, some, picks, starts=None):
        return project(
            [[sided(k, a)] for a in some],
            picks,
            jnp.stack([side_chunks[a] for a in some]),
            chunk_width,
            weights,
            starts,
        )

    for k in range(half, late - 1):
        send_until(place[k, rear] + 2)
        q, kv = far_block(k, range(chunks), jnp.stack([side]))
        hold[place[k + 1, front] + 2] = kv
        sources.append((q, kv, 0, lambda b, zz, k=k: (b == zz + k) | (b == zz - k)))
    send_until(place[late - 1, rear])
    begun = far_block(late - 1, range(chunks - 1), jnp.stack([side]))
    hold[place[late, middle]] = begun[1]
    send_until(place[late, middle])

    def home(way, k, c):
        x, first = piece_at(way, k, c)
        return x, first + home_offset

    slots = [([(tokens, z * width_share)], z, z >= 0)]
    for k in range(1, half):
        slots.append(([home(down, k, c) for c in range(chunks)], z + k, z + k < n))
        slots.append(([home(up, k, c) for c in range(chunks)], z - k, z >= k))
    for k in range(half, late):
        from_both = [home(down, k, c) for c in range(chunks // 2)]
        from_both += [home(up, k, c) for c in range(chunks // 2, chunks)]
        slots.append((from_both, jnp.where(side == 0, z + k, z - k), (z + k < n) | (z >= k)))
    slots.append(([(last_in[front], home_offset)], jnp.where(side == 0, late, 0), (z == 0) | (z == late)))
    low_part = low_parts(
        slots, after(home_chunk, last_out[middle]), width_share, packed, members
    )
    hold[len(turns) - 1] = low_part
    send_until(len(turns))
    low = low_part.astype(F32)
    for r in range(1, n):
        low += lax.ppermute(low_part, "tensor", [(i, (i + r) % n) for i in range(n)]).astype(F32)
    low = low.astype(BF16)
    q, kv = far_block(late - 1, [chunks - 1], after(jnp.stack([side]), low_part), begun)
    sources.append((q, kv, 0, lambda b, zz: (b == zz + late - 1) | (b == zz - late + 1)))
    front_in, middle_in, back_in = (last_in[piece] for piece in (front, middle, rear))

    group_size = QUERY_HEADS // KEY_VALUE_HEADS
    head_local = query_width // HEAD_SIZE
    pair_heads = keyval_width // HEAD_SIZE
    used = max(head_local // group_size, 1)

    def first_used(rank):
        return rank * head_local // group_size - rank // 2 * pair_heads

    partner = z ^ 1
    cuts = (first_used(z), first_used(partner), used)
    query, mine, send, up_query, up_keyval = finish(
        sources,
        z,
        low,
        members,
        packed,
        (cosine, sine, key_cosine, key_sine),
        cuts,
        n,
    )
    recv = lax.ppermute(send, "tensor", [(i, i ^ 1) for i in range(n)])
    late_q, late_kv = project(
        [[[(front_in, 0)]]] + [[[(middle_in, a * chunk_width)]] for a in range(chunks - 2)],
        after(jnp.zeros((1,), jnp.int32), low_part),
        jnp.stack([side_chunks[0]] + list(range(1, chunks - 1))),
        chunk_width,
        weights,
    )

    late_block = jnp.where(side == 0, n - 1, 0)
    late_args = dict(
        piece=back_in, chunk_id=side_chunks[chunks - 1]
    )
    late_low = block_of(low, late_block)
    late_member = block_of(members, late_block)
    mine_late, send_late = finish_late(
        **late_args,
        weight=key_value_weight,
        sums=late_kv,
        low=late_low[:, ADAPTER_RANK:],
        member=late_member,
        up=up_keyval,
        cosine=block_of(key_cosine, late_block),
        sine=block_of(key_sine, late_block),
        cuts=cuts,
    )
    recv_late = lax.ppermute(send_late, "tensor", [(0, 1), (n - 1, n - 2)])
    (query_late,) = finish_late(
        **late_args,
        weight=query_weight,
        sums=late_q,
        low=late_low[:, :ADAPTER_RANK],
        member=late_member,
        up=up_query,
        cosine=block_of(cosine, late_block),
        sine=block_of(sine, late_block),
    )
    nowhere = jnp.int32(-1)
    own_late = jnp.where(z == 0, (n - 1) * rows, jnp.where(z == n - 1, 0, nowhere))
    partner_late = jnp.where(partner == 0, (n - 1) * rows, jnp.where(partner == n - 1, 0, nowhere))
    info = jnp.stack([own_late, partner_late, holds_keys.astype(jnp.int32)]).astype(jnp.int32)
    return attend(
        query,
        query_late,
        mine,
        mine_late,
        recv,
        recv_late,
        segment_row[:, None],
        segment_row[None, :],
        info,
        n,
    )


def solution(mesh):
    return jax.shard_map(
        on_device,
        mesh=mesh,
        in_specs=(
            P(("groups", "store", "tensor"), None),
            P(None, "tensor"),
            P(None, "tensor"),
            P("store", None, "tensor"),
            P("store", None, "tensor"),
            P("store", None, "tensor"),
            P("groups"),
            P("groups", None),
            P(("groups", "store"), None),
        ),
        out_specs=P(("groups", "store"), "tensor"),
        check_vma=False,
    )
```

```python
import functools
import math

import jax
import jax.numpy as jnp
from jax import lax
from jax.experimental import pallas as pl
from jax.experimental.pallas import tpu as pltpu
from jax.sharding import PartitionSpec as P

QUERY_HEADS = 64
KEY_VALUE_HEADS = 8
HEAD_SIZE = 128
ADAPTER_RANK = 64
STORE_REQUESTS = 4
LONGEST_REQUEST = 256

adapter_scale = 2.0
rope_theta = 500000.0

CHUNKS = 4
TILE = 128
MIB = 2**20
F32 = jnp.float32
BF16 = jnp.bfloat16
ANY = pl.BlockSpec(memory_space=pl.ANY)


def after(arrays, *others):
    return lax.optimization_barrier((arrays, others))[0]


def params(held):
    return pltpu.CompilerParams(vmem_limit_bytes=max(int(held) + 8 * MIB, 58 * MIB))


def whole(shape):
    return pl.BlockSpec(shape, lambda *_: (0,) * len(shape))


def unique(arrays):
    kept, places = [], []
    for x in arrays:
        at = next((i for i, y in enumerate(kept) if y is x), len(kept))
        if at == len(kept):
            kept.append(x)
        places.append(at)
    return kept, places


def start_picked(candidates, pick, width, target, semaphore):
    def start(source, first):
        pltpu.make_async_copy(source.at[:, pl.ds(first, width)], target, semaphore).start()

    if len(candidates) == 1:
        start(*candidates[0])
        return
    for index, (source, first) in enumerate(candidates):
        pl.when(pick == index)(functools.partial(start, source, first))


def pack(down_maps, up_query, up_keyval, local):
    stores = local.shape[0]
    _, down_rows, width = down_maps.shape
    _, rank, keyval_width = up_keyval.shape
    cut = width // keyval_width
    strip = rank // cut

    height = down_rows + rank + strip

    def kernel(rows, down_ref, upq_ref, upkv_ref, *rest):
        outs, (held, sems, out_sems) = rest[:stores], rest[stores:]
        copies, writes = [], []
        for d in range(stores):
            here = held.at[d]
            sources = [
                (down_ref.at[rows[d]], here.at[pl.ds(0, down_rows), :]),
                (upq_ref.at[rows[d]], here.at[pl.ds(down_rows, rank), :]),
            ]
            for i in range(cut):
                sources.append(
                    (
                        upkv_ref.at[rows[d], pl.ds(i * strip, strip), :],
                        here.at[
                            pl.ds(down_rows + rank, strip), pl.ds(i * keyval_width, keyval_width)
                        ],
                    )
                )
            copies.append(
                [
                    pltpu.make_async_copy(source, target, sems.at[d, i])
                    for i, (source, target) in enumerate(sources)
                ]
            )
            writes.append(pltpu.make_async_copy(here, outs[d], out_sems.at[d]))
        for group in copies:
            for copy in group:
                copy.start()
        for group, write in zip(copies, writes):
            for copy in group:
                copy.wait()
            write.start()
        for write in writes:
            write.wait()

    return pl.pallas_call(
        kernel,
        grid_spec=pltpu.PrefetchScalarGridSpec(
            num_scalar_prefetch=1,
            grid=(1,),
            in_specs=[ANY] * 3,
            out_specs=[ANY] * stores,
            scratch_shapes=[
                pltpu.VMEM((stores, height, width), BF16),
                pltpu.SemaphoreType.DMA((stores, 2 + cut)),
                pltpu.SemaphoreType.DMA((stores,)),
            ],
        ),
        out_shape=[jax.ShapeDtypeStruct((height, width), BF16)] * stores,
        compiler_params=params(2 * stores * height * width),
    )(local, down_maps, up_query, up_keyval)


def project(candidates, picks, chunk_ids, chunk, weights, starts=None, start_group=0):
    steps, groups = len(candidates), len(candidates[0])
    rows = next(x.shape[0] for group in candidates[0] for x, _ in group)
    block = min(1024, chunk)
    sub = chunk // block
    blocks = steps * sub
    ahead = min(3, blocks)
    arrays, places = unique([x for a in candidates for group in a for x, _ in group])
    widths = [w.shape[1] for w in weights]
    count = len(weights)
    height = groups * rows

    def kernel(info, *refs):
        place = iter(places)
        sources = [[[(refs[next(place)], c) for _, c in group] for group in a] for a in candidates]
        rest = refs[len(arrays) :]
        weight_refs, rest = rest[:count], rest[count:]
        if starts is not None:
            start_refs, rest = rest[:count], rest[count:]
        out_refs, rest = rest[:count], rest[count:]
        streams, (held, sems, stream_sems) = rest[:count], rest[count:]

        def loads(i, slot):
            at = info[groups + i // sub] * sub + i % sub
            here = pl.ds(pl.multiple_of(at * block, block), block)
            return [
                pltpu.make_async_copy(
                    weight_refs[w].at[here, :], streams[w].at[slot], stream_sems.at[slot, w]
                )
                for w in range(count)
            ]

        for a in range(steps):
            for r in range(groups):
                target = held.at[a, pl.ds(r * rows, rows), :]
                if sources[a][r]:
                    start_picked(sources[a][r], info[r], chunk, target, sems.at[a, r])
                else:
                    target[...] = jnp.zeros(target.shape, BF16)
            if a == 0:
                for i in range(ahead):
                    for load in loads(i, i):
                        load.start()
        for w in range(count):
            out_refs[w][...] = jnp.zeros_like(out_refs[w]) if starts is None else start_refs[w][...]

        def body(i, carry):
            slot = lax.rem(i, ahead)
            at, part_at = i // sub, lax.rem(i, sub)

            for r in range(groups):
                here = [a for a in range(steps) if sources[a][r]]
                first_piece = part_at == 0
                if len(here) < steps:
                    first_piece &= functools.reduce(jnp.logical_or, [at == a for a in here])

                @pl.when(first_piece)
                def _(r=r, source=sources[here[0]][r][0][0]):
                    pltpu.make_async_copy(
                        source.at[:, pl.ds(0, chunk)],
                        held.at[at, pl.ds(r * rows, rows), :],
                        sems.at[at, r],
                    ).wait()

            for load in loads(i, slot):
                load.wait()
            part = held[at, :, pl.ds(pl.multiple_of(part_at * block, block), block)]
            for w in range(count):
                out_refs[w][...] += jnp.dot(
                    part, streams[w][slot], preferred_element_type=F32
                )

            @pl.when(i + ahead < blocks)
            def _():
                for load in loads(i + ahead, slot):
                    load.start()

            return carry

        lax.fori_loop(0, blocks, body, 0)

    info = jnp.concatenate([jnp.asarray(picks, jnp.int32), jnp.asarray(chunk_ids, jnp.int32)])
    return pl.pallas_call(
        kernel,
        grid_spec=pltpu.PrefetchScalarGridSpec(
            num_scalar_prefetch=1,
            grid=(1,),
            in_specs=[ANY] * (len(arrays) + count)
            + (
                [pl.BlockSpec((height, w), lambda g, info: (start_group, 0)) for w in widths]
                if starts is not None
                else []
            ),
            out_specs=[whole((height, w)) for w in widths],
            scratch_shapes=[pltpu.VMEM((ahead, block, w), BF16) for w in widths]
            + [
                pltpu.VMEM((steps, height, chunk), BF16),
                pltpu.SemaphoreType.DMA((steps, groups)),
                pltpu.SemaphoreType.DMA((ahead, count)),
            ],
        ),
        out_shape=[jax.ShapeDtypeStruct((height, w), F32) for w in widths],
        compiler_params=params(
            2 * steps * height * chunk + (2 * ahead * block + 16 * height) * sum(widths)
        ),
        cost_estimate=pl.CostEstimate(
            flops=2 * height * steps * chunk * sum(widths),
            bytes_accessed=2 * steps * chunk * (sum(widths) + height),
            transcendentals=0,
        ),
    )(info, *arrays, *weights, *(starts or []))


def low_parts(slots, pick, width, packed, members):
    arrays, places = unique([x for group, _, _ in slots for x, _ in group])
    count, holders = len(slots), len(packed)
    rows = arrays[0].shape[0]
    total = members.shape[0]
    rank = 2 * ADAPTER_RANK
    firsts = jnp.stack([jnp.asarray(c, jnp.int32) for group, _, _ in slots for _, c in group])
    info = jnp.concatenate(
        [
            jnp.stack([pick]),
            jnp.stack([b for _, b, _ in slots]),
            jnp.stack([v.astype(jnp.int32) for _, _, v in slots]),
            firsts,
        ]
    ).astype(jnp.int32)

    def kernel(info, *refs):
        place = iter(enumerate(places))
        sources = []
        for group, _, _ in slots:
            at = [next(place) for _ in group]
            sources.append(
                [(refs[p], pl.multiple_of(info[1 + 2 * count + i], HEAD_SIZE)) for i, p in at]
            )
        pack_refs = refs[len(arrays) : len(arrays) + holders]
        member_ref, out_ref, held, maps, sems, map_sems = refs[len(arrays) + holders :]
        loads = [
            pltpu.make_async_copy(
                pack_refs[d].at[pl.ds(0, rank), :],
                maps.at[pl.ds(d * rank, rank), :],
                map_sems.at[d],
            )
            for d in range(holders)
        ]
        for load in loads:
            load.start()
        for i in range(count):
            pl.when(info[1 + count + i] == 1)(
                functools.partial(
                    start_picked, sources[i], info[0], width, held.at[i], sems.at[i]
                )
            )
        for load in loads:
            load.wait()
        for i in range(count):

            @pl.when(info[1 + count + i] == 1)
            def _(i=i):
                pltpu.make_async_copy(
                    sources[i][0][0].at[:, pl.ds(0, width)], held.at[i], sems.at[i]
                ).wait()
                here = pl.ds(pl.multiple_of(info[1 + i] * rows, rows), rows)
                member = member_ref[here, :]
                product = lax.dot_general(
                    held[i], maps[...], (((1,), (1,)), ((), ())), preferred_element_type=F32
                )
                sum_ = product[:, :rank] * member[:, 0:1]
                for d in range(1, holders):
                    sum_ += product[:, d * rank : (d + 1) * rank] * member[:, d : d + 1]
                out_ref[here, :] = sum_.astype(BF16)

    return pl.pallas_call(
        kernel,
        grid_spec=pltpu.PrefetchScalarGridSpec(
            num_scalar_prefetch=1,
            grid=(1,),
            in_specs=[ANY] * (len(arrays) + holders) + [whole(members.shape)],
            out_specs=whole((total, rank)),
            scratch_shapes=[
                pltpu.VMEM((count, rows, width), BF16),
                pltpu.VMEM((holders * rank, width), BF16),
                pltpu.SemaphoreType.DMA((count,)),
                pltpu.SemaphoreType.DMA((holders,)),
            ],
        ),
        out_shape=jax.ShapeDtypeStruct((total, rank), BF16),
        compiler_params=params(
            2 * count * rows * width
            + 4 * holders * packed[0].size
            + 16 * total * HEAD_SIZE
        ),
        cost_estimate=pl.CostEstimate(
            flops=2 * total * width * rank * holders,
            bytes_accessed=2 * width * (total + rank * holders),
            transcendentals=0,
        ),
    )(info, *arrays, *packed, members)


def spread(low, member):
    return jnp.concatenate([low * member[:, d : d + 1] for d in range(member.shape[1])], axis=1)


def rotate(block, cosine, sine):
    return block * cosine + pltpu.roll(block, HEAD_SIZE // 2, 1) * sine


def finish(sources, rank_index, low, members, packed, tables, firsts, blocks):
    rows = low.shape[0] // blocks
    query_width = sources[0][0].shape[1]
    keyval_width = sources[0][1].shape[1]
    used = firsts[2] * HEAD_SIZE
    rank = ADAPTER_RANK
    count = len(sources)
    holders = len(packed)
    cut = query_width // keyval_width
    strip = rank // cut
    sums_in, places = unique([x for q, kv, _, _ in sources for x in (q, kv)])

    def kernel(info, *refs):
        sums = [refs[p] for p in places]
        rest = refs[len(sums_in) :]
        pack_refs, rest = rest[:holders], rest[holders:]
        low_ref, member_ref, cos_ref, sin_ref, kcos_ref, ksin_ref = rest[:6]
        query_ref, mine_ref, send_ref, upq_ref, upkv_ref = rest[6:11]
        held_q, held_kv, turned, sems, up_sems = rest[11:]
        block = pl.program_id(0)
        z = info[0]

        def loads(b, i):
            first = sources[i][2]
            return [
                pltpu.make_async_copy(
                    sums[2 * i + j].at[pl.ds(first, rows), :], held.at[b], sems.at[b, j]
                )
                for j, held in enumerate((held_q, held_kv))
            ]

        ups = []
        for d, packed_ref in enumerate(pack_refs):
            at = d * rank
            ups.append(
                (packed_ref.at[pl.ds(2 * rank, rank), :], upq_ref.at[pl.ds(at, rank), :])
            )
            for i in range(cut):
                ups.append(
                    (
                        packed_ref.at[
                            pl.ds(3 * rank, strip), pl.ds(i * keyval_width, keyval_width)
                        ],
                        upkv_ref.at[pl.ds(at + i * strip, strip), :],
                    )
                )
        ups = [pltpu.make_async_copy(a, b, up_sems.at[i]) for i, (a, b) in enumerate(ups)]

        @pl.when(block == 0)
        def _():
            for b in range(blocks):
                for i, (_, _, _, test) in enumerate(sources):

                    @pl.when(test(b, z))
                    def _(b=b, i=i):
                        for load in loads(b, i):
                            load.start()

            for load in ups:
                load.start()
            for load in ups:
                load.wait()

        def add_and_turn(b):
            member = member_ref[...].astype(BF16)
            low_block = low_ref[...]
            update = jnp.dot(
                spread(low_block[:, :rank], member), upq_ref[...], preferred_element_type=F32
            )
            for h in range(query_width // HEAD_SIZE):
                at = slice(h * HEAD_SIZE, (h + 1) * HEAD_SIZE)
                query_ref[:, at] = rotate(
                    held_q[b, :, at] + adapter_scale * update[:, at], cos_ref[...], sin_ref[...]
                ).astype(BF16)
            update = jnp.dot(
                spread(low_block[:, rank:], member), upkv_ref[...], preferred_element_type=F32
            )
            for h in range(keyval_width // HEAD_SIZE):
                at = slice(h * HEAD_SIZE, (h + 1) * HEAD_SIZE)
                turned[:, at] = rotate(
                    held_kv[b, :, at] + adapter_scale * update[:, at], kcos_ref[...], ksin_ref[...]
                )
            for out, first in ((mine_ref, info[1]), (send_ref, info[2])):
                out[...] = turned[:, pl.ds(pl.multiple_of(first, HEAD_SIZE), used)].astype(BF16)

        there = functools.reduce(jnp.logical_or, [test(block, z) for _, _, _, test in sources])

        @pl.when(there)
        def _():
            for load in loads(block, 0):
                load.wait()
            add_and_turn(block)

    def by_block(width):
        return pl.BlockSpec((rows, width), lambda b, info: (b, 0))

    total = rows * blocks
    info = jnp.stack([rank_index, firsts[0] * HEAD_SIZE, firsts[1] * HEAD_SIZE]).astype(jnp.int32)
    return pl.pallas_call(
        kernel,
        grid_spec=pltpu.PrefetchScalarGridSpec(
            num_scalar_prefetch=1,
            grid=(blocks,),
            in_specs=[ANY] * (len(sums_in) + holders)
            + [by_block(low.shape[1]), by_block(members.shape[1])]
            + [by_block(HEAD_SIZE)] * 4,
            out_specs=[
                by_block(query_width),
                by_block(used),
                by_block(used),
                whole((holders * rank, query_width)),
                whole((holders * rank, keyval_width)),
            ],
            scratch_shapes=[
                pltpu.VMEM((blocks, rows, query_width), F32),
                pltpu.VMEM((blocks, rows, keyval_width), F32),
                pltpu.VMEM((rows, keyval_width), F32),
                pltpu.SemaphoreType.DMA((blocks, 2)),
                pltpu.SemaphoreType.DMA((holders * (1 + cut),)),
            ],
        ),
        out_shape=[
            jax.ShapeDtypeStruct((total, query_width), BF16),
            jax.ShapeDtypeStruct((total, used), BF16),
            jax.ShapeDtypeStruct((total, used), BF16),
            jax.ShapeDtypeStruct((holders * rank, query_width), BF16),
            jax.ShapeDtypeStruct((holders * rank, keyval_width), BF16),
        ],
        compiler_params=params(
            (4 * total + 12 * rows + 4 * holders * rank) * (query_width + keyval_width)
        ),
        cost_estimate=pl.CostEstimate(
            flops=2 * total * holders * rank * (query_width + keyval_width),
            bytes_accessed=8 * total * (query_width + keyval_width),
            transcendentals=0,
        ),
    )(info, *sums_in, *packed, low, members, *tables)


def finish_late(piece, chunk_id, weight, sums, low, member, up, cosine, sine, cuts=None):
    rows, chunk = piece.shape
    width = weight.shape[1]
    step_width = min(1024, width)
    steps = width // step_width

    def kernel(info, x_ref, weight_ref, sum_ref, low_ref, member_ref, up_ref, cos_ref, sin_ref, *outs):
        update = jnp.dot(
            spread(low_ref[...], member_ref[...].astype(BF16)),
            up_ref[...],
            preferred_element_type=F32,
        )
        raw = (
            jnp.dot(x_ref[...], weight_ref[...], preferred_element_type=F32)
            + sum_ref[...]
            + adapter_scale * update
        )
        parts = [
            rotate(raw[:, h * HEAD_SIZE : (h + 1) * HEAD_SIZE], cos_ref[...], sin_ref[...])
            for h in range(step_width // HEAD_SIZE)
        ]
        if cuts is None:
            for h, part in enumerate(parts):
                outs[0][:, h * HEAD_SIZE : (h + 1) * HEAD_SIZE] = part.astype(BF16)
        else:
            for out, first in ((outs[0], info[1]), (outs[1], info[2])):
                for u in range(cuts[2]):
                    chosen = parts[0]
                    for h in range(1, len(parts)):
                        chosen = jnp.where(first + u == h, parts[h], chosen)
                    out[:, u * HEAD_SIZE : (u + 1) * HEAD_SIZE] = chosen.astype(BF16)

    def column(height):
        return pl.BlockSpec((height, step_width), lambda g, info: (0, g))

    if cuts is None:
        outs = [jax.ShapeDtypeStruct((rows, width), BF16)]
        out_specs = [column(rows)]
        info = [chunk_id]
    else:
        used = cuts[2] * HEAD_SIZE
        outs = [jax.ShapeDtypeStruct((rows, used), BF16)] * 2
        out_specs = [whole((rows, used))] * 2
        info = [chunk_id, cuts[0], cuts[1]]
    return pl.pallas_call(
        kernel,
        grid_spec=pltpu.PrefetchScalarGridSpec(
            num_scalar_prefetch=1,
            grid=(steps,),
            in_specs=[
                whole(piece.shape),
                pl.BlockSpec((chunk, step_width), lambda g, info: (info[0], g)),
                column(rows),
                whole(low.shape),
                whole(member.shape),
                column(up.shape[0]),
                whole(cosine.shape),
                whole(sine.shape),
            ],
            out_specs=out_specs,
        ),
        out_shape=outs,
        compiler_params=params(4 * (chunk + up.shape[0] + 4 * rows) * step_width + 4 * rows * chunk),
        cost_estimate=pl.CostEstimate(
            flops=2 * rows * width * (chunk + up.shape[0]),
            bytes_accessed=2 * width * chunk,
            transcendentals=0,
        ),
    )(jnp.stack(info).astype(jnp.int32), piece, weight, sums, low, member, up, cosine, sine)


def attend(query, query_late, mine, mine_late, recv, recv_late, ids_column, ids_row, info, blocks):
    total, width = query.shape
    rows = total // blocks
    heads = width // HEAD_SIZE
    used = mine.shape[1] // HEAD_SIZE
    per_kv = heads // used
    together = min(8, per_kv)
    span = together * HEAD_SIZE
    scale = math.log2(math.e) / math.sqrt(HEAD_SIZE)
    tiles = total // TILE
    back = -(-(LONGEST_REQUEST - 1) // TILE)

    longest = (back + 1) * TILE

    def kernel(info, q_ref, ql_ref, m_ref, ml_ref, r_ref, rl_ref, idc_ref, idr_ref, out_ref, *held):
        k_ref, v_ref, bias_ref, held_q = held
        step = pl.program_id(0)

        @pl.when(step == 0)
        def _():
            def put(keys_mine):
                own, other = (k_ref, v_ref) if keys_mine else (v_ref, k_ref)
                own[...] = m_ref[...]
                other[...] = r_ref[...]

                @pl.when(info[0] >= 0)
                def _():
                    own[pl.ds(pl.multiple_of(info[0], rows), rows), :] = ml_ref[...]

                @pl.when(info[1] >= 0)
                def _():
                    other[pl.ds(pl.multiple_of(info[1], rows), rows), :] = rl_ref[...]

            pl.when(info[2] == 1)(lambda: put(True))
            pl.when(info[2] == 0)(lambda: put(False))
            for tile in range(tiles):
                first = max(0, tile - back) * TILE
                size = (tile + 1) * TILE - first
                row_index = lax.broadcasted_iota(jnp.int32, (TILE, size), 0) + tile * TILE
                key_index = lax.broadcasted_iota(jnp.int32, (TILE, size), 1) + first
                same = idc_ref[tile * TILE : (tile + 1) * TILE, :] == idr_ref[:, first : first + size]
                bias_ref[tile, :, :size] = jnp.where(same & (row_index >= key_index), 0.0, -1e30)

        held_q[...] = q_ref[...]

        @pl.when(info[0] >= 0)
        def _():
            held_q[pl.ds(pl.multiple_of(info[0], rows), rows), :] = ql_ref[...]

        kv_at = pl.ds(pl.multiple_of((step * together // per_kv) * HEAD_SIZE, HEAD_SIZE), HEAD_SIZE)
        for tile in range(tiles):
            first = max(0, tile - back) * TILE
            size = (tile + 1) * TILE - first
            at = slice(tile * TILE, (tile + 1) * TILE)
            keys = k_ref[first : first + size, kv_at]
            values = v_ref[first : first + size, kv_at]
            values = jnp.concatenate([values, jnp.ones_like(values)], axis=1)
            queries = jnp.concatenate(
                [held_q[at, h * HEAD_SIZE : (h + 1) * HEAD_SIZE] for h in range(together)], axis=0
            )
            scores = lax.dot_general(
                queries, keys, (((1,), (1,)), ((), ())), preferred_element_type=F32
            ).reshape(together, TILE, size)
            scores = scores * scale + bias_ref[tile, :, :size][None]
            top = jnp.max(scores, axis=2, keepdims=True)
            weights = jnp.exp2(scores - top).astype(BF16).reshape(together * TILE, size)
            mixed = jnp.dot(weights, values, preferred_element_type=F32)
            mixed = (mixed[:, :HEAD_SIZE] / mixed[:, HEAD_SIZE:]).astype(BF16)
            for h in range(together):
                out_ref[at, h * HEAD_SIZE : (h + 1) * HEAD_SIZE] = mixed[h * TILE : (h + 1) * TILE]

    by_heads = pl.BlockSpec((total, span), lambda g, info: (0, g))
    return pl.pallas_call(
        kernel,
        grid_spec=pltpu.PrefetchScalarGridSpec(
            num_scalar_prefetch=1,
            grid=(heads // together,),
            in_specs=[
                by_heads,
                pl.BlockSpec((rows, span), lambda g, info: (0, g)),
                whole(mine.shape),
                whole(mine_late.shape),
                whole(recv.shape),
                whole(recv_late.shape),
                whole(ids_column.shape),
                whole(ids_row.shape),
            ],
            out_specs=by_heads,
            scratch_shapes=[
                pltpu.VMEM(mine.shape, BF16),
                pltpu.VMEM(mine.shape, BF16),
                pltpu.VMEM((tiles, TILE, longest), F32),
                pltpu.VMEM((total, span), BF16),
            ],
        ),
        out_shape=jax.ShapeDtypeStruct((total, width), BF16),
        compiler_params=params(8 * total * span + 12 * mine.size + 4 * MIB),
        cost_estimate=pl.CostEstimate(
            flops=4 * total * total * width,
            bytes_accessed=4 * total * width,
            transcendentals=total * total * heads,
        ),
    )(info, query, query_late, mine, mine_late, recv, recv_late, ids_column, ids_row)


def on_device(
    tokens,
    query_weight,
    key_value_weight,
    adapter_down_maps,
    adapter_up_query,
    adapter_up_key_value,
    adapter_row_table,
    request_adapter_ids,
    token_request_ids,
):
    z = lax.axis_index("tensor")
    store = lax.axis_index("store")
    n = lax.axis_size("tensor")
    stores = lax.axis_size("store")
    rows, model_width = tokens.shape
    total = rows * n
    half = n // 2
    late = n - 1
    chunks = CHUNKS
    chunk_width = model_width // chunks
    width_share = model_width // n
    slices = n // chunks
    home_chunk = z // slices
    home_offset = (z % slices) * width_share
    side = (z >= half).astype(jnp.int32)
    query_width = query_weight.shape[1]
    keyval_width = key_value_weight.shape[1]

    front, middle, rear = (0, 1), (1, chunks - 1), (chunks - 1, chunks)
    turns = [(k, piece) for k in range(1, n) for piece in (front, middle, rear)]
    at = turns.index((late, front))
    turns[at - 1], turns[at] = turns[at], turns[at - 1]
    place = {turn: i for i, turn in enumerate(turns)}
    down = {(0, (0, chunks)): tokens}
    up = dict(down)

    def mirrored(piece):
        return (chunks - piece[1], chunks - piece[0])

    def piece_at(way, k, chunk):
        for (j, (first, end)), x in way.items():
            if j == k and first <= chunk < end:
                return x, (chunk - first) * chunk_width

    def cut_out(way, k, piece):
        x, first = piece_at(way, k, piece[0])
        wide = (piece[1] - piece[0]) * chunk_width
        return x if x.shape[1] == wide else x[:, first : first + wide]

    came = {}

    def send_turn(i, *others):
        k, piece = turns[i]
        other_piece = mirrored(piece)
        if i >= 2:
            others += came[i - 2]
        sends = (cut_out(down, k - 1, piece), cut_out(up, k - 1, other_piece))
        if k == late:
            send = after(jnp.where(side == 0, *sends), *others)
            last_out[piece] = send
            came[i] = (lax.ppermute(send, "tensor", [(1, 0), (n - 2, n - 1)]),)
            last_in[piece] = came[i][0]
            return
        if i == 0:
            first_sends.extend(sends)
        if i == 1:
            others += tuple(first_sends)
        send_down, send_up = after(sends, *others)
        if i == 1:
            first_sends.extend((send_down, send_up))
        down[k, piece] = lax.ppermute(
            send_down, "tensor", [(j, j - 1) for j in range(1, n - k + 1)]
        )
        up[k, other_piece] = lax.ppermute(
            send_up, "tensor", [(j, j + 1) for j in range(k - 1, n - 1)]
        )
        came[i] = (down[k, piece], up[k, other_piece])

    hold = {}
    first_sends = []
    last_in, last_out = {}, {}
    next_turn = 0

    def send_until(turn):
        nonlocal next_turn
        while next_turn <= min(turn, len(turns) - 1):
            send_turn(next_turn, *([hold[next_turn]] if next_turn in hold else []))
            next_turn += 1

    send_until(1)

    per_store = adapter_down_maps.shape[0]
    lookup = (
        request_adapter_ids[:, :, None]
        == jnp.arange(adapter_row_table.shape[0], dtype=jnp.int32)[None, None, :]
    ).astype(jnp.int32)
    slot_table = jnp.sum(lookup * adapter_row_table[None, None, :], axis=2)
    here = slot_table // per_store == store
    local = jnp.sum(jnp.where(here, slot_table - store * per_store, 0), axis=1)

    packed = pack(
        adapter_down_maps,
        adapter_up_query,
        adapter_up_key_value,
        after(
            lax.dynamic_slice_in_dim(jnp.concatenate([local, local]), store, stores, 0), *first_sends
        ),
    )
    packed = list(packed)
    for d in range(1, stores):
        packed[d] = lax.ppermute(
            after(packed[d], packed[d - 1]), "store", [(i, (i + d) % stores) for i in range(stores)]
        )

    segment_row = token_request_ids[0]
    my_holders = lax.dynamic_index_in_dim(slot_table, store, 0, keepdims=False) // per_store
    requests = jnp.arange(STORE_REQUESTS, dtype=jnp.int32)
    holder_order = (store - jnp.arange(stores, dtype=jnp.int32)) % stores
    served = jnp.max(
        jnp.where(my_holders[None, :] == holder_order[:, None], requests[None, :], -1), axis=1
    )
    members = (segment_row[:, None] == served[None, :]).astype(F32)
    starts = jnp.sum((segment_row[:, None] < requests[None, :]).astype(jnp.int32), axis=0)
    first_index = jnp.sum(
        jnp.where(segment_row[:, None] == requests[None, :], starts[None, :], 0), axis=1
    )
    positions = jnp.arange(total, dtype=jnp.int32) - first_index
    exponent = jnp.arange(HEAD_SIZE // 2, dtype=F32) * (2.0 / HEAD_SIZE)
    frequency = jnp.exp(-exponent * math.log(rope_theta))
    angles = positions.astype(F32)[:, None] * frequency[None, :]
    cosine, sine = jnp.cos(angles), jnp.sin(angles)
    cosine = jnp.concatenate([cosine, cosine], axis=1)
    sine = jnp.concatenate([-sine, sine], axis=1)
    holds_keys = z % 2 == 0
    key_cosine = jnp.where(holds_keys, cosine, 1.0)
    key_sine = jnp.where(holds_keys, sine, 0.0)

    def block_of(array, index):
        return lax.dynamic_slice_in_dim(array, jnp.clip(index, 0, n - 1) * rows, rows, 0)

    weights = [query_weight, key_value_weight]
    sources = []
    side_chunks = [jnp.where(side == 0, a, chunks - 1 - a) for a in range(chunks)]

    def sided(k, a):
        return [piece_at(down, k, a), piece_at(up, k, chunks - 1 - a)]

    for k in range(1, half):
        send_until(place[k, rear] + 2)
        ways = ([(down, 0)] if k == 1 else []) + [(down, k), (up, k)]
        q, kv = project(
            [[[piece_at(way, j, c)] for way, j in ways] for c in range(chunks)],
            jnp.zeros((len(ways),), jnp.int32),
            list(range(chunks)),
            chunk_width,
            weights,
        )
        hold[place[k + 1, front] + 2] = kv
        first = 0
        if k == 1:
            sources.append((q, kv, 0, lambda b, zz: b == zz))
            first = rows
        sources.append((q, kv, first, lambda b, zz, k=k: b == zz + k))
        sources.append((q, kv, first + rows, lambda b, zz, k=k: b == zz - k))

    for k in range(half, late - 1):
        send_until(place[k, rear] + 2)
        q, kv = project(
            [[sided(k, a)] for a in range(chunks)],
            jnp.stack([side]),
            jnp.stack(side_chunks),
            chunk_width,
            weights,
        )
        hold[place[k + 1, front] + 2] = kv
        sources.append((q, kv, 0, lambda b, zz, k=k: (b == zz + k) | (b == zz - k)))
    send_until(place[late, middle])

    def home(way, k, c):
        x, first = piece_at(way, k, c)
        return x, first + home_offset

    slots = [([(tokens, z * width_share)], z, z >= 0)]
    for k in range(1, half):
        slots.append(([home(down, k, c) for c in range(chunks)], z + k, z + k < n))
        slots.append(([home(up, k, c) for c in range(chunks)], z - k, z >= k))
    for k in range(half, late):
        from_both = [home(down, k, c) for c in range(chunks // 2)]
        from_both += [home(up, k, c) for c in range(chunks // 2, chunks)]
        slots.append((from_both, jnp.where(side == 0, z + k, z - k), (z + k < n) | (z >= k)))
    slots.append(([(last_in[front], home_offset)], jnp.where(side == 0, late, 0), (z == 0) | (z == late)))
    low_part = low_parts(
        slots, after(home_chunk, last_out[middle]), width_share, packed, members
    )
    hold[len(turns) - 1] = low_part
    send_until(len(turns))
    low = low_part.astype(F32)
    for r in range(1, n):
        low += lax.ppermute(low_part, "tensor", [(i, (i + r) % n) for i in range(n)]).astype(F32)
    low = low.astype(BF16)
    front_in, middle_in, back_in = (last_in[piece] for piece in (front, middle, rear))
    q, kv = project(
        [[sided(late - 1, a), [(front_in, 0)] if a == 0 else []] for a in range(chunks)],
        after(jnp.stack([side, side]), low_part),
        jnp.stack(side_chunks),
        chunk_width,
        weights,
    )
    late_begun = [q, kv]
    sources.append((q, kv, 0, lambda b, zz: (b == zz + late - 1) | (b == zz - late + 1)))

    group_size = QUERY_HEADS // KEY_VALUE_HEADS
    head_local = query_width // HEAD_SIZE
    pair_heads = keyval_width // HEAD_SIZE
    used = max(head_local // group_size, 1)

    def first_used(rank):
        return rank * head_local // group_size - rank // 2 * pair_heads

    partner = z ^ 1
    cuts = (first_used(z), first_used(partner), used)
    query, mine, send, up_query, up_keyval = finish(
        sources,
        z,
        low,
        members,
        packed,
        (cosine, sine, key_cosine, key_sine),
        cuts,
        n,
    )
    recv = lax.ppermute(send, "tensor", [(i, i ^ 1) for i in range(n)])
    late_q, late_kv = project(
        [[[(middle_in, a * chunk_width)]] for a in range(chunks - 2)],
        after(jnp.zeros((1,), jnp.int32), mine),
        jnp.arange(1, chunks - 1, dtype=jnp.int32),
        chunk_width,
        weights,
        late_begun,
        1,
    )

    late_block = jnp.where(side == 0, n - 1, 0)
    late_args = dict(
        piece=back_in, chunk_id=side_chunks[chunks - 1]
    )
    late_low = block_of(low, late_block)
    late_member = block_of(members, late_block)
    mine_late, send_late = finish_late(
        **late_args,
        weight=key_value_weight,
        sums=late_kv,
        low=late_low[:, ADAPTER_RANK:],
        member=late_member,
        up=up_keyval,
        cosine=block_of(key_cosine, late_block),
        sine=block_of(key_sine, late_block),
        cuts=cuts,
    )
    recv_late = lax.ppermute(send_late, "tensor", [(0, 1), (n - 1, n - 2)])
    (query_late,) = finish_late(
        **late_args,
        weight=query_weight,
        sums=late_q,
        low=late_low[:, :ADAPTER_RANK],
        member=late_member,
        up=up_query,
        cosine=block_of(cosine, late_block),
        sine=block_of(sine, late_block),
    )
    nowhere = jnp.int32(-1)
    own_late = jnp.where(z == 0, (n - 1) * rows, jnp.where(z == n - 1, 0, nowhere))
    partner_late = jnp.where(partner == 0, (n - 1) * rows, jnp.where(partner == n - 1, 0, nowhere))
    info = jnp.stack([own_late, partner_late, holds_keys.astype(jnp.int32)]).astype(jnp.int32)
    return attend(
        query,
        query_late,
        mine,
        mine_late,
        recv,
        recv_late,
        segment_row[:, None],
        segment_row[None, :],
        info,
        n,
    )


def solution(mesh):
    return jax.shard_map(
        on_device,
        mesh=mesh,
        in_specs=(
            P(("groups", "store", "tensor"), None),
            P(None, "tensor"),
            P(None, "tensor"),
            P("store", None, "tensor"),
            P("store", None, "tensor"),
            P("store", None, "tensor"),
            P("groups"),
            P("groups", None),
            P(("groups", "store"), None),
        ),
        out_specs=P(("groups", "store"), "tensor"),
        check_vma=False,
    )
```
